512 devices in a mesh: dp: 32 (over x_hi, y, core), expert: 16 (over z, x_lo).
Axes of the slice: x: 4 (x_hi: 2, x_lo: 2; x = x_hi * 2 + x_lo), y: 8, z: 8, core: 2. Of those that a mesh axis runs over, the one named last changes fastest.
Arguments:
- tokens: bfloat16 [512, 256, 1408], P(('dp', 'expert')), may hold values from -12 to 12
- cotangent: bfloat16 [512, 256, 1408], P(('dp', 'expert')), may hold values from -6 to 6
- slot_outputs: bfloat16 [512, 16, 1408], P(('dp', 'expert')), may hold values from -0.29882812 to 0.29882812
- slot_params: bfloat16 [1408, 16], replicated, may hold values from -0.5 to 0.5
- lift_weight: bfloat16 [16, 6144, 1408], P('expert', 'dp'), may hold values from -0.15625 to 0.15625
- drop_weight: bfloat16 [16, 6144, 1408], P('expert', 'dp'), may hold values from -0.078125 to 0.078125
Outputs:
- token_grad: bfloat16 [512, 256, 1408], P(('dp', 'expert'))
- param_grad: float32 [1408, 16], replicated
- lift_grad: bfloat16 [16, 6144, 1408], P('expert', 'dp')
- drop_grad: bfloat16 [16, 6144, 1408], P('expert', 'dp')
The draws below stay inside these ranges and needn't reach their ends.
All inputs are finite; a program needn't handle non-finite values.
Results may differ from the reference program's by a relative error of at most 0.04.
Values may be sent and summed in bfloat16 or wider, within the bound.
No kernel may reach another device: no remote copies, remote signals or barrier semaphores. Data moves between devices by JAX's collectives and lax.ppermute only.
A program may use at most 64 MiB of HBM per device.

```python
import math
import jax
import jax.numpy as jnp
from jax import lax

D = 1408
FF = 6144
P_SIZE = 256
EXPERTS = 16
IMAGES = 512
N_DP = 32


def draw_tokens(key, part):
    key = jax.random.fold_in(key, 3)
    first = jax.random.fold_in(key, 0)
    return jnp.clip(jax.random.normal(first, (IMAGES, P_SIZE, D), jnp.float32), -6.0, 6.0).astype(jnp.bfloat16)


def draw_slot_params(key, part):
    key = jax.random.fold_in(key, 5)
    first = jax.random.fold_in(key, 0)
    noise = jax.random.normal(first, (D, EXPERTS), jnp.float32) * (1.5 / math.sqrt(D))
    return jnp.clip(noise, -0.5, 0.5).astype(jnp.bfloat16)


def steps_of(own_key, shape, pieces, low, high):
    def one(axis_at, shards_of):
        steps = jax.random.uniform(jax.random.fold_in(jax.random.fold_in(own_key, 6), axis_at), (shards_of,), jnp.float32, low / len(pieces), high / len(pieces))
        return jnp.repeat(jnp.exp(steps), shape[axis_at] // shards_of).reshape((-1,) + (1,) * (len(shape) - axis_at - 1))

    gain = one(*pieces[0])
    for cut in pieces[1:]:
        gain = gain * one(*cut)
    return gain


def normal_values(own_key, extent, width, bound, cuts=(), held_as=jnp.bfloat16):
    result = jax.random.normal(own_key, extent, jnp.float32) * width
    if len(cuts) > 0:
        result = steps_of(own_key, extent, cuts, -0.22, 0.18) * result
    return jnp.clip(result, min=-bound, max=bound).astype(held_as)


def setup_inputs(seed: int = 0) -> dict:
    seeds = jax.random.split(jax.random.key(seed), 7)
    tokens = draw_tokens(jax.random.fold_in(seeds[6], 71), 0)
    cotangent = normal_values(seeds[1], (IMAGES, P_SIZE, D), 1.0, 6.0, ((0, 512),))
    slot_outputs = normal_values(seeds[2], (IMAGES, EXPERTS, D), 0.05, 0.29882812, ((0, 512),))
    slot_params = draw_slot_params(jax.random.fold_in(seeds[6], 71), 0)
    lift_weight = normal_values(seeds[4], (EXPERTS, FF, D), D ** -0.5, 0.15625, ((0, 16), (1, 32)))
    drop_weight = normal_values(seeds[5], (EXPERTS, FF, D), FF ** -0.5, 0.078125, ((0, 16), (1, 32)))
    return {"tokens": tokens, "cotangent": cotangent, "slot_outputs": slot_outputs, "slot_params": slot_params, "lift_weight": lift_weight, "drop_weight": drop_weight}


def gelu_value(values):
    return 0.5 * values * (1.0 + jax.scipy.special.erf(values * 0.7071067811865476))


def gelu_slope(values):
    return 0.5 * (1.0 + jax.scipy.special.erf(values * 0.7071067811865476)) + values * jnp.exp(-0.5 * values * values) * 0.3989422804014327


def reference(tokens, cotangent, slot_outputs, slot_params, lift_weight, drop_weight):
    highest_precision_mode = lax.Precision.HIGHEST
    token_rows_wide = tokens.astype(jnp.float32)
    upstream_wide = cotangent.astype(jnp.float32)
    params_wide = slot_params.astype(jnp.float32)
    logits = jnp.einsum("bpd,ds->bps", token_rows_wide, params_wide, precision=highest_precision_mode)
    dispatch = jax.nn.softmax(logits, axis=1)
    combine_weight_rows = jax.nn.softmax(logits, axis=2)
    dispatch_half = dispatch.astype(jnp.bfloat16)
    combine_half = combine_weight_rows.astype(jnp.bfloat16)
    slot_input_rows = jnp.einsum("bps,bpd->bsd", dispatch_half.astype(jnp.float32), token_rows_wide, precision=highest_precision_mode).astype(jnp.bfloat16)
    slot_upstream = jnp.einsum("bps,bpd->bsd", combine_half.astype(jnp.float32), upstream_wide, precision=highest_precision_mode).astype(jnp.bfloat16)
    combine_grad = jnp.einsum("bpd,bsd->bps", upstream_wide, slot_outputs.astype(jnp.float32), precision=highest_precision_mode)
    group_width = FF // N_DP

    def per_expert(operands):
        inputs, upstream, lift, drop = operands
        preact = jnp.dot(inputs, lift.T, preferred_element_type=jnp.float32)
        activated = gelu_value(preact).astype(jnp.bfloat16)
        activated_grad = jnp.dot(upstream, drop.T, preferred_element_type=jnp.float32)
        preact_grad = (activated_grad * gelu_slope(preact)).astype(jnp.bfloat16)
        drop_sum = jnp.dot(activated.T, upstream, preferred_element_type=jnp.float32).astype(jnp.bfloat16)
        lift_sum = jnp.dot(preact_grad.T, inputs, preferred_element_type=jnp.float32).astype(jnp.bfloat16)
        gradient_by_group = preact_grad.astype(jnp.float32).reshape(preact_grad.shape[0], N_DP, group_width)
        lift_by_group = lift.astype(jnp.float32).reshape(N_DP, group_width, lift.shape[1])
        slice_parts = jnp.einsum("wat,ati->wai", gradient_by_group, lift_by_group, precision=highest_precision_mode).astype(jnp.bfloat16)
        backward = jnp.sum(slice_parts.astype(jnp.float32), axis=1).astype(jnp.bfloat16)
        return lift_sum, drop_sum, backward

    lift_grad, drop_grad, backward = lax.map(per_expert, (jnp.swapaxes(slot_input_rows, 0, 1), jnp.swapaxes(slot_upstream, 0, 1), lift_weight, drop_weight))
    slot_grad = jnp.swapaxes(backward, 0, 1).astype(jnp.float32)
    dispatch_grad = jnp.einsum("bpd,bsd->bps", token_rows_wide, slot_grad, precision=highest_precision_mode)
    logits_gradient = combine_weight_rows * (combine_grad - jnp.sum(combine_grad * combine_weight_rows, axis=2, keepdims=True))
    logits_gradient = logits_gradient + dispatch * (dispatch_grad - jnp.sum(dispatch_grad * dispatch, axis=1, keepdims=True))
    param_grad = jnp.einsum("bpd,bps->ds", token_rows_wide, logits_gradient, precision=highest_precision_mode)
    token_grad = jnp.einsum("bps,bsd->bpd", dispatch_half.astype(jnp.float32), slot_grad, precision=highest_precision_mode)
    token_grad = token_grad + jnp.einsum("bps,ds->bpd", logits_gradient, params_wide, precision=highest_precision_mode)
    return token_grad.astype(jnp.bfloat16), param_grad, lift_grad, drop_grad
```

```python
import jax
import jax.numpy as jnp
from jax import lax
from jax.sharding import Mesh, PartitionSpec as P

AXES = ("xhi", "y", "core", "z", "xlo")
DP = ("xhi", "y", "core")
EXPERT = ("z", "xlo")
HIDDEN = ("y", "z", "xlo")
SWAP = [(0, 1), (1, 0)]
BF16 = jnp.bfloat16
F32 = jnp.float32


def gelu_value(values):
    return 0.5 * values * (1.0 + jax.scipy.special.erf(values * 0.7071067811865476))


def gelu_slope(values):
    return (
        0.5 * (1.0 + jax.scipy.special.erf(values * 0.7071067811865476))
        + values * jnp.exp(-0.5 * values * values) * 0.3989422804014327
    )


def mm(spec, a, b):
    return jnp.einsum(spec, a, b, preferred_element_type=F32)


def fold(rows):
    head = rows[:, :768]
    tail = jnp.pad(rows[:, 768:], ((0, 0), (0, 128)))
    return jnp.stack([head, tail], axis=1)


def unfold(blocks):
    return jnp.concatenate([blocks[:, 0, :], blocks[:, 1, :640]], axis=1)


def exchange(blocks, axes):
    return lax.all_to_all(blocks, axes, split_axis=0, concat_axis=0, tiled=True)


def split_float(values):
    high = values.astype(BF16)
    return high, (values - high.astype(F32)).astype(BF16)


def shards(tokens, cotangent, slot_outputs, slot_params, lift_weight, drop_weight):
    tokens, cotangent, slot_outputs = tokens[0], cotangent[0], slot_outputs[0]
    own = jnp.concatenate([lift_weight[0], drop_weight[0]], axis=0)
    over_x = lax.ppermute(own, "xhi", SWAP)
    over_core = lax.ppermute(own, "core", SWAP)
    over_both = lax.ppermute(over_x, "core", SWAP)

    params_t = slot_params.T
    logits = mm("sd,pd->sp", params_t, tokens)
    dispatch = jax.nn.softmax(logits, axis=1)
    combine = jax.nn.softmax(logits, axis=0)
    dispatch_half = dispatch.astype(BF16)
    slot_inputs = mm("sp,pd->sd", dispatch_half, tokens).astype(BF16)
    slot_upstream = mm("sp,pd->sd", combine.astype(BF16), cotangent).astype(BF16)
    sent = jnp.stack([slot_inputs, slot_upstream], axis=1)
    sent = jnp.broadcast_to(sent[None], (8, 16, 2, 1408)).reshape(128, 2, 1408)
    routed = exchange(sent, HIDDEN)
    inputs, upstream = routed[:, 0, :], routed[:, 1, :]

    combine_grad = mm("sd,pd->sp", slot_outputs, cotangent)
    combine_part = combine * (
        combine_grad - jnp.sum(combine_grad * combine, axis=0, keepdims=True)
    )

    hidden = []
    backward = None
    for block in (own, over_x, over_core, over_both):
        lift, drop = block[:192], block[192:]
        preact = mm("nd,fd->nf", inputs, lift)
        activated_grad = mm("nd,fd->nf", upstream, drop)
        activated = gelu_value(preact).astype(BF16)
        preact_grad = (activated_grad * gelu_slope(preact)).astype(BF16)
        hidden.append((activated, preact_grad))
        part = mm("nf,fd->nd", preact_grad, lift)
        backward = part if backward is None else backward + part
    returned = exchange(fold(backward.astype(BF16)), HIDDEN)
    slot_grad = jnp.sum(returned.astype(F32).reshape(8, 16, 2, 768), axis=0)
    slot_grad = unfold(slot_grad.astype(BF16))

    sums = [
        jnp.concatenate(
            [mm("nf,nd->fd", preact_grad, inputs), mm("nf,nd->fd", activated, upstream)], axis=0
        )
        for activated, preact_grad in hidden
    ]
    from_core = lax.ppermute(
        jnp.concatenate([sums[2], sums[3]], axis=0).astype(BF16), "core", SWAP
    ).astype(F32)
    from_x = lax.ppermute((sums[1] + from_core[384:]).astype(BF16), "xhi", SWAP)
    weight_grads = (sums[0] + from_core[:384] + from_x.astype(F32)).astype(BF16)

    dispatch_grad = mm("sd,pd->sp", slot_grad, tokens)
    logit_grad = combine_part + dispatch * (
        dispatch_grad - jnp.sum(dispatch_grad * dispatch, axis=1, keepdims=True)
    )
    high, low = split_float(logit_grad)
    local = mm("sp,pd->sd", jnp.concatenate([high, low], axis=0), tokens)
    local = local[:16] + local[16:]
    by_slot = exchange(fold(local.astype(BF16)), EXPERT)
    by_slot = jnp.sum(by_slot.astype(F32), axis=0).astype(BF16)
    by_group = exchange(jnp.broadcast_to(by_slot[None], (32, 2, 768)), DP)
    total = jnp.sum(by_group.astype(F32), axis=0).astype(BF16)
    columns = exchange(jnp.broadcast_to(total[None], (16, 2, 768)), EXPERT)
    param_grad = unfold(columns).astype(F32).T

    token_grad = mm(
        "kp,kd->pd",
        jnp.concatenate([dispatch_half, high, low], axis=0),
        jnp.concatenate([slot_grad, params_t, params_t], axis=0),
    ).astype(BF16)
    return (token_grad[None], param_grad, weight_grads[None, :192], weight_grads[None, 192:])


def solution(mesh):
    split = Mesh(mesh.devices.reshape(2, 8, 2, 8, 2), AXES)
    images = P(AXES, None, None)
    hidden = P(EXPERT, DP, None)
    return jax.shard_map(
        shards,
        mesh=split,
        in_specs=(images, images, images, P(), hidden, hidden),
        out_specs=(images, P(), hidden, hidden),
        check_vma=False,
    )
```

```python
import jax
import jax.numpy as jnp
from jax import lax
from jax.experimental import pallas as pl
from jax.experimental.pallas import tpu as pltpu
from jax.sharding import Mesh, PartitionSpec as P

AXES = ("xhi", "y", "core", "z", "xlo")
DP = ("xhi", "y", "core")
NEAR = ("core", "z")
FAR = ("xhi", "y", "xlo")
EXPERT = ("z", "xlo")
HIDDEN = ("y", "z", "xlo")
SWAP = [(0, 1), (1, 0)]
BF16 = jnp.bfloat16
F32 = jnp.float32


def mm(spec, a, b):
    return jnp.einsum(spec, a, b, preferred_element_type=F32)


def dot(a, b, contract):
    return lax.dot_general(a, b, (contract, ((), ())), preferred_element_type=F32)


def call(kernel, out, args, macs):
    return pl.pallas_call(
        kernel,
        out_shape=out,
        in_specs=[pl.BlockSpec(memory_space=pltpu.VMEM)] * len(args),
        out_specs=jax.tree.map(lambda _: pl.BlockSpec(memory_space=pltpu.VMEM), out),
        compiler_params=pltpu.CompilerParams(vmem_limit_bytes=40 * 2**20),
        cost_estimate=pl.CostEstimate(
            flops=2 * macs,
            bytes_accessed=sum(a.size * a.dtype.itemsize for a in list(args) + list(out)),
            transcendentals=0,
        ),
    )(*args)


def hidden_kernel(x_ref, g_ref, w0, w1, w2, w3, back_ref, act_ref, slope_ref):
    total = None
    for k, w in enumerate((w0, w1, w2, w3)):
        lift = w[:192, :]
        preact = dot(lift, x_ref[...], ((1,), (1,)))
        activated_grad = dot(w[192:, :], g_ref[...], ((1,), (1,)))
        rise = 0.5 * (1.0 + lax.erf(preact * 0.7071067811865476))
        bell = preact * jnp.exp(-0.5 * preact * preact) * 0.3989422804014327
        act_ref[pl.ds(192 * k, 192), :] = (preact * rise).astype(BF16)
        preact_grad = (activated_grad * (rise + bell)).astype(BF16)
        slope_ref[pl.ds(192 * k, 192), :] = preact_grad
        part = dot(preact_grad, lift, ((0,), (0,)))
        total = part if total is None else total + part
    back_ref[...] = total.astype(BF16)


def block_grads(k, x_ref, g_ref, act_ref, slope_ref):
    rows = pl.ds(192 * k, 192)
    lift = dot(slope_ref[rows, :], x_ref[...], ((1,), (0,)))
    drop = dot(act_ref[rows, :], g_ref[...], ((1,), (0,)))
    return lift, drop


def copy_kernel(src_ref, dst_ref):
    dst_ref[...] = src_ref[...]


def core_kernel(x_ref, g_ref, act_ref, slope_ref, out_ref):
    for k in (2, 3):
        lift, drop = block_grads(k, x_ref, g_ref, act_ref, slope_ref)
        out_ref[pl.ds(384 * (k - 2), 192), :] = lift.astype(BF16)
        out_ref[pl.ds(384 * (k - 2) + 192, 192), :] = drop.astype(BF16)


def x_kernel(x_ref, g_ref, act_ref, slope_ref, core_ref, out_ref):
    lift, drop = block_grads(1, x_ref, g_ref, act_ref, slope_ref)
    out_ref[:192, :] = (lift + core_ref[384:576, :].astype(F32)).astype(BF16)
    out_ref[192:, :] = (drop + core_ref[576:, :].astype(F32)).astype(BF16)


def own_kernel(x_ref, g_ref, act_ref, slope_ref, core_ref, over_ref, lift_ref, drop_ref):
    lift, drop = block_grads(0, x_ref, g_ref, act_ref, slope_ref)
    lift_ref[...] = (
        lift + core_ref[:192, :].astype(F32) + over_ref[:192, :].astype(F32)
    ).astype(BF16)
    drop_ref[...] = (
        drop + core_ref[192:384, :].astype(F32) + over_ref[192:, :].astype(F32)
    ).astype(BF16)


def fold(rows):
    head = rows[:, :768]
    tail = jnp.pad(rows[:, 768:], ((0, 0), (0, 128)))
    return jnp.stack([head, tail], axis=1)


def unfold(blocks):
    return jnp.concatenate([blocks[:, 0, :], blocks[:, 1, :640]], axis=1)


def exchange(blocks, axes):
    return lax.all_to_all(blocks, axes, split_axis=0, concat_axis=0, tiled=True)


def split_float(values):
    high = values.astype(BF16)
    return high, (values - high.astype(F32)).astype(BF16)


def shards(tokens, cotangent, slot_outputs, slot_params, lift_weight, drop_weight):
    tokens, cotangent, slot_outputs = tokens[0], cotangent[0], slot_outputs[0]
    own = jnp.concatenate([lift_weight[0], drop_weight[0]], axis=0)
    over_x = lax.ppermute(own, "xhi", SWAP)
    over_core = lax.ppermute(own, "core", SWAP)
    over_x = pl.pallas_call(
        copy_kernel,
        out_shape=jax.ShapeDtypeStruct((384, 1408), BF16),
        cost_estimate=pl.CostEstimate(flops=2 * 10**10, bytes_accessed=4, transcendentals=0),
    )(over_x)
    over_both = lax.ppermute(over_x, "core", SWAP)

    params_t = slot_params.T
    logits = mm("sd,pd->sp", params_t, tokens)
    dispatch = jax.nn.softmax(logits, axis=1)
    combine = jax.nn.softmax(logits, axis=0)
    dispatch_half = dispatch.astype(BF16)
    slot_inputs = mm("sp,pd->sd", dispatch_half, tokens).astype(BF16)
    slot_upstream = mm("sp,pd->sd", combine.astype(BF16), cotangent).astype(BF16)
    sent = jnp.stack([slot_inputs, slot_upstream], axis=1)
    sent = jnp.broadcast_to(sent[None], (8, 16, 2, 1408)).reshape(128, 2, 1408)
    routed = exchange(sent, HIDDEN)
    inputs, upstream = routed[:, 0, :], routed[:, 1, :]

    combine_grad = mm("sd,pd->sp", slot_outputs, cotangent)
    combine_part = combine * (
        combine_grad - jnp.sum(combine_grad * combine, axis=0, keepdims=True)
    )

    shape = jax.ShapeDtypeStruct
    units = shape((768, 128), BF16)
    backward, activated, slopes = call(
        hidden_kernel,
        (shape((128, 1408), BF16), units, units),
        (inputs, upstream, own, over_x, over_core, over_both),
        3 * 128 * 768 * 1408,
    )
    returned = exchange(fold(backward), HIDDEN)
    slot_grad = jnp.sum(returned.astype(F32).reshape(8, 16, 2, 768), axis=0)
    slot_grad = unfold(slot_grad.astype(BF16))

    rows = (inputs, upstream, activated, slopes)
    to_core = call(core_kernel, (shape((768, 1408), BF16),), rows, 4 * 192 * 128 * 1408)[0]
    from_core = lax.ppermute(to_core, "core", SWAP)
    to_x = call(
        x_kernel, (shape((384, 1408), BF16),), rows + (from_core,), 2 * 192 * 128 * 1408
    )[0]
    from_x = lax.ppermute(to_x, "xhi", SWAP)
    half = shape((192, 1408), BF16)
    lift_grad, drop_grad = call(
        own_kernel, (half, half), rows + (from_core, from_x), 2 * 192 * 128 * 1408
    )

    dispatch_grad = mm("sd,pd->sp", slot_grad, tokens)
    logit_grad = combine_part + dispatch * (
        dispatch_grad - jnp.sum(dispatch_grad * dispatch, axis=1, keepdims=True)
    )
    high, low = split_float(logit_grad)
    local = mm("sp,pd->sd", jnp.concatenate([high, low], axis=0), tokens)
    local = local[:16] + local[16:]
    by_slot = exchange(fold(local.astype(BF16)), NEAR)
    by_slot = jnp.sum(by_slot.astype(F32), axis=0).astype(BF16)
    by_group = exchange(jnp.broadcast_to(by_slot[None], (32, 2, 768)), FAR)
    total = jnp.sum(by_group.astype(F32), axis=0).astype(BF16)
    columns = exchange(jnp.broadcast_to(total[None], (16, 2, 768)), NEAR)
    param_grad = unfold(columns).astype(F32).T

    token_grad = mm(
        "kp,kd->pd",
        jnp.concatenate([dispatch_half, high, low], axis=0),
        jnp.concatenate([slot_grad, params_t, params_t], axis=0),
    ).astype(BF16)
    return (token_grad[None], param_grad, lift_grad[None], drop_grad[None])


def solution(mesh):
    split = Mesh(mesh.devices.reshape(2, 8, 2, 8, 2), AXES)
    images = P(AXES, None, None)
    hidden = P(EXPERT, DP, None)
    return jax.shard_map(
        shards,
        mesh=split,
        in_specs=(images, images, images, P(), hidden, hidden),
        out_specs=(images, P(), hidden, hidden),
        check_vma=False,
    )
```

```python
import jax
import jax.numpy as jnp
from jax import lax
from jax.experimental import pallas as pl
from jax.experimental.pallas import tpu as pltpu
from jax.sharding import Mesh, PartitionSpec as P

AXES = ("xhi", "y", "core", "z", "xlo")
DP = ("xhi", "y", "core")
NEAR = ("core", "z")
FAR = ("xhi", "y", "xlo")
EXPERT = ("z", "xlo")
HIDDEN = ("y", "z", "xlo")
SWAP = [(0, 1), (1, 0)]
BF16 = jnp.bfloat16
F32 = jnp.float32


def mm(spec, a, b):
    return jnp.einsum(spec, a, b, preferred_element_type=F32)


def dot(a, b, contract):
    return lax.dot_general(a, b, (contract, ((), ())), preferred_element_type=F32)


def specs(args):
    return [
        pl.BlockSpec(memory_space=pltpu.SMEM if a.ndim == 1 else pltpu.VMEM) for a in args
    ]


def call(kernel, out, args, macs):
    return pl.pallas_call(
        kernel,
        out_shape=out,
        in_specs=specs(args),
        out_specs=jax.tree.map(lambda _: pl.BlockSpec(memory_space=pltpu.VMEM), out),
        compiler_params=pltpu.CompilerParams(vmem_limit_bytes=16 * 2**20),
        cost_estimate=pl.CostEstimate(
            flops=2 * macs,
            bytes_accessed=sum(a.size * a.dtype.itemsize for a in list(args) + list(out)),
            transcendentals=0,
        ),
    )(*args)


def softmax(values, axis):
    top = jnp.exp(values - jnp.max(values, axis=axis, keepdims=True))
    return top / jnp.sum(top, axis=axis, keepdims=True)


def route_kernel(low, tok, cot, par, kept_ref, away_ref, dispatch_ref, combine_ref):
    logits = dot(par[...], tok[...], ((1,), (1,)))
    dispatch_ref[...] = softmax(logits, 1)
    combine_ref[...] = softmax(logits, 0)
    row = lax.broadcasted_iota(jnp.int32, (16, 16), 0)
    column = lax.broadcasted_iota(jnp.int32, (16, 16), 1)
    mine = 1 - low[0]
    wanted = jnp.where(row < 8, 2 * row + mine, 2 * (row - 8) + 1 - mine)
    order = jnp.where(column == wanted, 1.0, 0.0).astype(BF16)
    for k, (weights, rows) in enumerate(((dispatch_ref, tok), (combine_ref, cot))):
        both = dot(order, weights[...].astype(BF16), ((1,), (0,))).astype(BF16)
        sums = dot(both, rows[...], ((1,), (0,))).astype(BF16)
        kept_ref[:, k, :] = sums[:8, :]
        away_ref[:, k, :] = sums[8:, :]


def spread_kernel(low, kept, met, out, rows, sems):
    @pl.when(low[0] == 1)
    def _():
        rows[:, 0] = kept[...]
        rows[:, 1] = met[...]

    @pl.when(low[0] != 1)
    def _():
        rows[:, 0] = met[...]
        rows[:, 1] = kept[...]

    copies = [pltpu.make_async_copy(rows, out.at[y], sems.at[y]) for y in range(8)]
    for copy in copies:
        copy.start()
    for copy in copies:
        copy.wait()


def hidden_kernel(
    routed, w0, w1, w2, w3, back_ref, act_ref, slope_ref, x_ref, g_ref
):
    x_ref[...] = routed[:, 0, :]
    g_ref[...] = routed[:, 1, :]
    total = None
    for k, w in enumerate((w0, w1, w2, w3)):
        lift = w[:192, :]
        preact = dot(lift, x_ref[...], ((1,), (1,)))
        activated_grad = dot(w[192:, :], g_ref[...], ((1,), (1,)))
        rise = 0.5 * (1.0 + lax.erf(preact * 0.7071067811865476))
        bell = preact * jnp.exp(-0.5 * preact * preact) * 0.3989422804014327
        act_ref[pl.ds(192 * k, 192), :] = (preact * rise).astype(BF16)
        preact_grad = (activated_grad * (rise + bell)).astype(BF16)
        slope_ref[pl.ds(192 * k, 192), :] = preact_grad
        part = dot(preact_grad, lift, ((0,), (0,)))
        total = part if total is None else total + part
    back = total.astype(BF16)
    back_ref[:, 0, :] = back[:, :768]
    back_ref[:, 1, :640] = back[:, 768:]
    back_ref[:, 1, 640:] = jnp.zeros((128, 128), BF16)


def block_grads(k, x_ref, g_ref, act_ref, slope_ref):
    rows = pl.ds(192 * k, 192)
    lift = dot(slope_ref[rows, :], x_ref[...], ((1,), (0,)))
    drop = dot(act_ref[rows, :], g_ref[...], ((1,), (0,)))
    return lift, drop


def copy_kernel(src_ref, dst_ref):
    dst_ref[...] = src_ref[...]


def core_kernel(x_ref, g_ref, act_ref, slope_ref, out_ref):
    for k in (2, 3):
        lift, drop = block_grads(k, x_ref, g_ref, act_ref, slope_ref)
        out_ref[pl.ds(384 * (k - 2), 192), :] = lift.astype(BF16)
        out_ref[pl.ds(384 * (k - 2) + 192, 192), :] = drop.astype(BF16)


def x_kernel(x_ref, g_ref, act_ref, slope_ref, core_ref, out_ref):
    lift, drop = block_grads(1, x_ref, g_ref, act_ref, slope_ref)
    out_ref[:192, :] = (lift + core_ref[384:576, :].astype(F32)).astype(BF16)
    out_ref[192:, :] = (drop + core_ref[576:, :].astype(F32)).astype(BF16)


def own_kernel(x_ref, g_ref, act_ref, slope_ref, core_ref, over_ref, lift_ref, drop_ref):
    lift, drop = block_grads(0, x_ref, g_ref, act_ref, slope_ref)
    lift_ref[...] = (
        lift + core_ref[:192, :].astype(F32) + over_ref[:192, :].astype(F32)
    ).astype(BF16)
    drop_ref[...] = (
        drop + core_ref[192:384, :].astype(F32) + over_ref[192:, :].astype(F32)
    ).astype(BF16)


def fold(rows):
    head = rows[:, :768]
    tail = jnp.pad(rows[:, 768:], ((0, 0), (0, 128)))
    return jnp.stack([head, tail], axis=1)


def unfold(blocks):
    return jnp.concatenate([blocks[:, 0, :], blocks[:, 1, :640]], axis=1)


def exchange(blocks, axes):
    return lax.all_to_all(blocks, axes, split_axis=0, concat_axis=0, tiled=True)


def split_float(values):
    high = values.astype(BF16)
    return high, (values - high.astype(F32)).astype(BF16)


def shards(tokens, cotangent, slot_outputs, slot_params, lift_weight, drop_weight):
    tokens, cotangent, slot_outputs = tokens[0], cotangent[0], slot_outputs[0]
    own = jnp.concatenate([lift_weight[0], drop_weight[0]], axis=0)
    over_x = lax.ppermute(own, "xhi", SWAP)
    over_core = lax.ppermute(own, "core", SWAP)
    over_x = pl.pallas_call(
        copy_kernel,
        out_shape=jax.ShapeDtypeStruct((384, 1408), BF16),
        compiler_params=pltpu.CompilerParams(vmem_limit_bytes=16 * 2**20),
        cost_estimate=pl.CostEstimate(flops=2 * 10**10, bytes_accessed=4, transcendentals=0),
    )(over_x)
    over_both = lax.ppermute(over_x, "core", SWAP)

    params_t = slot_params.T
    low = (lax.axis_index("xlo") == 0).astype(jnp.int32).reshape(1)
    shape = jax.ShapeDtypeStruct
    rows = shape((8, 2, 1408), BF16)
    weights = shape((16, 256), F32)
    kept, away, dispatch, combine = call(
        route_kernel,
        (rows, rows, weights, weights),
        (low, tokens, cotangent, params_t),
        3 * 16 * 256 * 1408,
    )
    met = lax.ppermute(away, "xlo", SWAP)
    sent = pl.pallas_call(
        spread_kernel,
        out_shape=shape((8, 8, 2, 2, 1408), BF16),
        in_specs=specs((low, kept, met)),
        out_specs=pl.BlockSpec(memory_space=pltpu.HBM),
        scratch_shapes=[pltpu.VMEM((8, 2, 2, 1408), BF16), pltpu.SemaphoreType.DMA((8,))],
        compiler_params=pltpu.CompilerParams(vmem_limit_bytes=16 * 2**20),
        cost_estimate=pl.CostEstimate(flops=0, bytes_accessed=10**6, transcendentals=0),
    )(low, kept, met)
    routed = exchange(sent.reshape(128, 2, 1408), ("y", "z"))
    dispatch_half = dispatch.astype(BF16)

    combine_grad = mm("sd,pd->sp", slot_outputs, cotangent)
    combine_part = combine * (
        combine_grad - jnp.sum(combine_grad * combine, axis=0, keepdims=True)
    )

    units = shape((768, 128), BF16)
    images = shape((128, 1408), BF16)
    backward, activated, slopes, inputs, upstream = call(
        hidden_kernel,
        (shape((128, 2, 768), BF16), units, units, images, images),
        (routed, own, over_x, over_core, over_both),
        3 * 128 * 768 * 1408,
    )
    returned = exchange(backward, HIDDEN)
    rows = (inputs, upstream, activated, slopes)
    to_core = call(core_kernel, (shape((768, 1408), BF16),), rows, 4 * 192 * 128 * 1408)[0]
    from_core = lax.ppermute(to_core, "core", SWAP)
    to_x = call(
        x_kernel, (shape((384, 1408), BF16),), rows + (from_core,), 2 * 192 * 128 * 1408
    )[0]
    from_x = lax.ppermute(to_x, "xhi", SWAP)
    returned, to_x = lax.optimization_barrier((returned, to_x))
    slot_grad = jnp.sum(returned.astype(F32).reshape(8, 16, 2, 768), axis=0)
    slot_grad = unfold(slot_grad.astype(BF16))

    half = shape((192, 1408), BF16)
    lift_grad, drop_grad = call(
        own_kernel, (half, half), rows + (from_core, from_x), 2 * 192 * 128 * 1408
    )

    dispatch_grad = mm("sd,pd->sp", slot_grad, tokens)
    logit_grad = combine_part + dispatch * (
        dispatch_grad - jnp.sum(dispatch_grad * dispatch, axis=1, keepdims=True)
    )
    high, low = split_float(logit_grad)
    local = mm("sp,pd->sd", jnp.concatenate([high, low], axis=0), tokens)
    local = local[:16] + local[16:]
    by_slot = exchange(fold(local.astype(BF16)), NEAR)
    by_slot = jnp.sum(by_slot.astype(F32), axis=0).astype(BF16)
    by_group = exchange(jnp.broadcast_to(by_slot[None], (32, 2, 768)), FAR)
    total = jnp.sum(by_group.astype(F32), axis=0).astype(BF16)
    columns = exchange(jnp.broadcast_to(total[None], (16, 2, 768)), NEAR)
    columns, lift_grad, drop_grad = lax.optimization_barrier((columns, lift_grad, drop_grad))
    param_grad = unfold(columns).astype(F32).T

    token_grad = mm(
        "kp,kd->pd",
        jnp.concatenate([dispatch_half, high, low], axis=0),
        jnp.concatenate([slot_grad, params_t, params_t], axis=0),
    ).astype(BF16)
    return (token_grad[None], param_grad, lift_grad[None], drop_grad[None])


def solution(mesh):
    split = Mesh(mesh.devices.reshape(2, 8, 2, 8, 2), AXES)
    images = P(AXES, None, None)
    hidden = P(EXPERT, DP, None)
    return jax.shard_map(
        shards,
        mesh=split,
        in_specs=(images, images, images, P(), hidden, hidden),
        out_specs=(images, P(), hidden, hidden),
        check_vma=False,
    )
```

```python
import jax
import jax.numpy as jnp
from jax import lax
from jax.experimental import pallas as pl
from jax.experimental.pallas import tpu as pltpu
from jax.sharding import Mesh, PartitionSpec as P

AXES = ("xhi", "y", "core", "z", "xlo")
DP = ("xhi", "y", "core")
NEAR = ("core", "z")
FAR = ("xhi", "y", "xlo")
EXPERT = ("z", "xlo")
HIDDEN = ("y", "z", "xlo")
SWAP = [(0, 1), (1, 0)]
BF16 = jnp.bfloat16
F32 = jnp.float32
LIMIT = 56 * 2**20
shape = jax.ShapeDtypeStruct


def dot(a, b, contract):
    return lax.dot_general(a, b, (contract, ((), ())), preferred_element_type=F32)


def call(kernel, out, args, macs, hbm=False, scratch=(), aliases={}):
    place = pl.ANY if hbm else pltpu.VMEM
    return pl.pallas_call(
        kernel,
        out_shape=out,
        in_specs=[pl.BlockSpec(memory_space=place)] * len(args),
        out_specs=jax.tree.map(lambda _: pl.BlockSpec(memory_space=place), out),
        scratch_shapes=scratch,
        input_output_aliases=aliases,
        compiler_params=pltpu.CompilerParams(vmem_limit_bytes=LIMIT),
        cost_estimate=pl.CostEstimate(
            flops=2 * macs,
            bytes_accessed=sum(a.size * a.dtype.itemsize for a in list(args) + list(out)),
            transcendentals=0,
        ),
    )(*args)


def hold_kernel(src_ref, dst_ref):
    pass


def hold(value):
    return call(hold_kernel, (value,), (value,), 10**10, hbm=True, aliases={0: 0})[0]


def exchange(blocks, axes):
    return lax.all_to_all(blocks, axes, split_axis=0, concat_axis=0, tiled=True)


def softmax(values, axis):
    top = jnp.exp(values - jnp.max(values, axis=axis, keepdims=True))
    return top / jnp.sum(top, axis=axis, keepdims=True)


def route_kernel(tok, cot, par, out, dispatch_ref, combine_ref, tok_v, cot_v, pairs, sems):
    loads = [
        pltpu.make_async_copy(tok, tok_v, sems.at[0]),
        pltpu.make_async_copy(cot, cot_v, sems.at[1]),
    ]
    for load in loads:
        load.start()
    loads[0].wait()
    logits = dot(par[...], tok_v[...], ((1,), (1,)))
    dispatch = softmax(logits, 1)
    combine = softmax(logits, 0)
    dispatch_ref[...] = dispatch
    combine_ref[...] = combine
    pairs[:, 0, :] = dot(dispatch.astype(BF16), tok_v[...], ((1,), (0,))).astype(BF16)
    loads[1].wait()
    pairs[:, 1, :] = dot(combine.astype(BF16), cot_v[...], ((1,), (0,))).astype(BF16)
    copies = [pltpu.make_async_copy(pairs, out.at[y], sems.at[2 + y]) for y in range(8)]
    for copy in copies:
        copy.start()
    for copy in copies:
        copy.wait()


def route(tokens, cotangent, params_t):
    hbm = pl.BlockSpec(memory_space=pl.ANY)
    vmem = pl.BlockSpec(memory_space=pltpu.VMEM)
    return pl.pallas_call(
        route_kernel,
        out_shape=(shape((8, 16, 2, 1408), BF16), shape((16, 256), F32), shape((16, 256), F32)),
        in_specs=[hbm, hbm, vmem],
        out_specs=(hbm, vmem, vmem),
        scratch_shapes=[
            pltpu.VMEM((256, 1408), BF16),
            pltpu.VMEM((256, 1408), BF16),
            pltpu.VMEM((16, 2, 1408), BF16),
            pltpu.SemaphoreType.DMA((10,)),
        ],
        compiler_params=pltpu.CompilerParams(vmem_limit_bytes=LIMIT),
        cost_estimate=pl.CostEstimate(flops=4 * 10**7, bytes_accessed=3 * 10**6, transcendentals=0),
    )(tokens, cotangent, params_t)


def hidden_kernel(*refs):
    routed, weights, outs, scratch = refs[0], refs[1:9], refs[9:15], refs[15:]
    back_out, core_out, act_out, slope_out, x_out, g_out = outs
    rows, lifts, drops, x, g, act, slope, back, core, sems = scratch
    unpack = pltpu.make_async_copy(routed, rows, sems.at[0])
    unpack.start()
    order = (2, 3, 0, 1)
    loads = {}
    for k in order:
        part = pl.ds(192 * k, 192)
        loads[k] = (
            pltpu.make_async_copy(weights[2 * k], lifts.at[part], sems.at[1 + 2 * k]),
            pltpu.make_async_copy(weights[2 * k + 1], drops.at[part], sems.at[2 + 2 * k]),
        )
        for load in loads[k]:
            load.start()
    stores = []

    def store(src, dst):
        copy = pltpu.make_async_copy(src, dst, sems.at[9 + len(stores)])
        copy.start()
        stores.append(copy)

    unpack.wait()
    x[...] = rows[:, 0, :]
    g[...] = rows[:, 1, :]
    store(x, x_out)
    store(g, g_out)
    for k in order:
        part = pl.ds(192 * k, 192)
        for load in loads[k]:
            load.wait()
        preact = dot(lifts[part, :], x[...], ((1,), (1,)))
        activated_grad = dot(drops[part, :], g[...], ((1,), (1,)))
        rise = 0.5 * (1.0 + lax.erf(preact * 0.7071067811865476))
        bell = preact * jnp.exp(-0.5 * preact * preact) * 0.3989422804014327
        activated = (preact * rise).astype(BF16)
        preact_grad = (activated_grad * (rise + bell)).astype(BF16)
        act[part, :] = activated
        slope[part, :] = preact_grad
        if k >= 2:
            half = pl.ds(384 * (k - 2), 384)
            core[pl.ds(384 * (k - 2), 192), :] = dot(preact_grad, x[...], ((1,), (0,))).astype(BF16)
            core[pl.ds(384 * (k - 2) + 192, 192), :] = dot(
                activated, g[...], ((1,), (0,))
            ).astype(BF16)
            store(core.at[half], core_out.at[half])
    store(act, act_out)
    store(slope, slope_out)
    total = dot(slope[...], lifts[...], ((0,), (0,))).astype(BF16)
    back[:, 0, :] = total[:, :768]
    back[:, 1, :640] = total[:, 768:]
    back[:, 1, 640:] = jnp.zeros((128, 128), BF16)
    store(back, back_out)
    for copy in stores:
        copy.wait()


def block_grads(k, x_ref, g_ref, act_ref, slope_ref):
    rows = pl.ds(192 * k, 192)
    lift = dot(slope_ref[rows, :], x_ref[...], ((1,), (0,)))
    drop = dot(act_ref[rows, :], g_ref[...], ((1,), (0,)))
    return lift, drop


def x_kernel(x_ref, g_ref, act_ref, slope_ref, core_ref, out_ref):
    lift, drop = block_grads(1, x_ref, g_ref, act_ref, slope_ref)
    out_ref[:192, :] = (lift + core_ref[384:576, :].astype(F32)).astype(BF16)
    out_ref[192:, :] = (drop + core_ref[576:, :].astype(F32)).astype(BF16)


def own_kernel(x_ref, g_ref, act_ref, slope_ref, core_ref, over_ref, lift_ref, drop_ref):
    lift, drop = block_grads(0, x_ref, g_ref, act_ref, slope_ref)
    lift_ref[...] = (
        lift + core_ref[:192, :].astype(F32) + over_ref[:192, :].astype(F32)
    ).astype(BF16)
    drop_ref[...] = (
        drop + core_ref[192:384, :].astype(F32) + over_ref[192:, :].astype(F32)
    ).astype(BF16)


def combine_kernel(out_ref, cot, combine, grad_ref):
    grad = dot(out_ref[...], cot[...], ((1,), (1,)))
    weighted = jnp.sum(grad * combine[...], axis=0, keepdims=True)
    grad_ref[...] = combine[...] * (grad - weighted)


def image_kernel(
    returned, tok, par, dispatch, part, out, left_ref, right_ref, parts, tok_v, sems
):
    loads = [
        pltpu.make_async_copy(returned, parts, sems.at[0]),
        pltpu.make_async_copy(tok, tok_v, sems.at[1]),
    ]
    for load in loads:
        load.start()
    left_ref[:16, :] = dispatch[...].astype(BF16)
    right_ref[16:32, :] = par[...]
    right_ref[32:, :] = par[...]
    loads[0].wait()
    head = tail = None
    for y in range(8):
        rows = pl.ds(16 * y, 16)
        one = parts[rows, 0, :].astype(F32)
        two = parts[rows, 1, :].astype(F32)
        head = one if head is None else head + one
        tail = two if tail is None else tail + two
    slot_grad = jnp.concatenate([head, tail[:, :640]], axis=1).astype(BF16)
    right_ref[:16, :] = slot_grad
    loads[1].wait()
    grad = dot(slot_grad, tok_v[...], ((1,), (1,)))
    weighted = jnp.sum(grad * dispatch[...], axis=1, keepdims=True)
    logit = part[...] + dispatch[...] * (grad - weighted)
    high = logit.astype(BF16)
    low = (logit - high.astype(F32)).astype(BF16)
    left_ref[16:32, :] = high
    left_ref[32:, :] = low
    local = dot(high, tok_v[...], ((1,), (0,))) + dot(low, tok_v[...], ((1,), (0,)))
    local = local.astype(BF16)
    out[:, 0, :] = local[:, :768]
    out[:, 1, :640] = local[:, 768:]
    out[:, 1, 640:] = jnp.zeros((16, 128), BF16)


def shards(tokens, cotangent, slot_outputs, slot_params, lift_weight, drop_weight):
    tokens, cotangent, slot_outputs = tokens[0], cotangent[0], slot_outputs[0]
    lift, drop = lift_weight[0], drop_weight[0]
    x_lift = hold(lax.ppermute(lift, "xhi", SWAP))
    x_lift, lift_later, drop_later = lax.optimization_barrier((x_lift, lift, drop))
    x_drop = lax.ppermute(drop_later, "xhi", SWAP)
    c_lift = lax.ppermute(lift_later, "core", SWAP)
    c_drop = lax.ppermute(drop_later, "core", SWAP)
    b_lift = lax.ppermute(x_lift, "core", SWAP)
    b_drop = lax.ppermute(x_drop, "core", SWAP)

    params_t = slot_params.T
    sent, dispatch, combine = route(tokens, cotangent, params_t)
    routed = exchange(sent.reshape(128, 2, 1408), HIDDEN)
    combine_part = call(
        combine_kernel,
        (shape((16, 256), F32),),
        (slot_outputs, cotangent, combine),
        16 * 256 * 1408,
    )[0]

    units = shape((768, 128), BF16)
    images = shape((128, 1408), BF16)
    core_half = shape((768, 1408), BF16)
    folded = shape((128, 2, 768), BF16)
    backward, to_core, activated, slopes, inputs, upstream = call(
        hidden_kernel,
        (folded, core_half, units, units, images, images),
        (routed, lift, drop, x_lift, x_drop, c_lift, c_drop, b_lift, b_drop),
        5 * 128 * 768 * 1408,
        hbm=True,
        scratch=[
            pltpu.VMEM(a.shape, BF16)
            for a in (
                routed, core_half, core_half, images, images, units, units, folded, core_half
            )
        ]
        + [pltpu.SemaphoreType.DMA((16,))],
    )
    returned = exchange(backward, HIDDEN)
    rows = (inputs, upstream, activated, slopes)
    from_core = lax.ppermute(to_core, "core", SWAP)
    to_x = call(
        x_kernel, (shape((384, 1408), BF16),), rows + (from_core,), 2 * 192 * 128 * 1408
    )[0]
    from_x = lax.ppermute(to_x, "xhi", SWAP)
    returned, to_x = lax.optimization_barrier((returned, to_x))
    half = shape((192, 1408), BF16)
    lift_grad, drop_grad = call(
        own_kernel, (half, half), rows + (from_core, from_x), 2 * 192 * 128 * 1408
    )

    vmem = pl.BlockSpec(memory_space=pltpu.VMEM)
    hbm = pl.BlockSpec(memory_space=pl.ANY)
    local, left, right = pl.pallas_call(
        image_kernel,
        out_shape=(shape((16, 2, 768), BF16), shape((48, 256), BF16), shape((48, 1408), BF16)),
        in_specs=[hbm, hbm, vmem, vmem, vmem],
        out_specs=(vmem, vmem, vmem),
        scratch_shapes=[
            pltpu.VMEM((128, 2, 768), BF16),
            pltpu.VMEM((256, 1408), BF16),
            pltpu.SemaphoreType.DMA((2,)),
        ],
        compiler_params=pltpu.CompilerParams(vmem_limit_bytes=LIMIT),
        cost_estimate=pl.CostEstimate(flops=4 * 10**7, bytes_accessed=2 * 10**6, transcendentals=0),
    )(returned, tokens, params_t, dispatch, combine_part)
    by_slot = exchange(local, NEAR)
    by_slot = jnp.sum(by_slot.astype(F32), axis=0).astype(BF16)
    by_group = exchange(jnp.broadcast_to(by_slot[None], (32, 2, 768)), FAR)
    total = jnp.sum(by_group.astype(F32), axis=0).astype(BF16)
    columns = exchange(jnp.broadcast_to(total[None], (16, 2, 768)), NEAR)
    columns, lift_grad, drop_grad = lax.optimization_barrier((columns, lift_grad, drop_grad))
    param_grad = jnp.concatenate([columns[:, 0, :], columns[:, 1, :640]], axis=1).astype(F32).T

    token_grad = jnp.einsum("kp,kd->pd", left, right, preferred_element_type=F32).astype(BF16)
    return (token_grad[None], param_grad, lift_grad[None], drop_grad[None])


def solution(mesh):
    split = Mesh(mesh.devices.reshape(2, 8, 2, 8, 2), AXES)
    images = P(AXES, None, None)
    hidden = P(EXPERT, DP, None)
    return jax.shard_map(
        shards,
        mesh=split,
        in_specs=(images, images, images, P(), hidden, hidden),
        out_specs=(images, P(), hidden, hidden),
        check_vma=False,
    )
```

```python
import jax
import jax.numpy as jnp
from jax import lax
from jax.experimental import pallas as pl
from jax.experimental.pallas import tpu as pltpu
from jax.sharding import Mesh, PartitionSpec as P

AXES = ("xhi", "y", "core", "z", "xlo")
DP = ("xhi", "y", "core")
NEAR = ("core", "z")
FAR = ("xhi", "y", "xlo")
EXPERT = ("z", "xlo")
HIDDEN = ("y", "z", "xlo")
SWAP = [(0, 1), (1, 0)]
BF16 = jnp.bfloat16
F32 = jnp.float32
LIMIT = 56 * 2**20
SMALL = 24 * 2**20
shape = jax.ShapeDtypeStruct


def dot(a, b, contract):
    return lax.dot_general(a, b, (contract, ((), ())), preferred_element_type=F32)


def call(kernel, out, args, macs, hbm=False, scratch=(), aliases={}, limit=LIMIT):
    place = pl.ANY if hbm else pltpu.VMEM
    return pl.pallas_call(
        kernel,
        out_shape=out,
        in_specs=[pl.BlockSpec(memory_space=place) for a in args],
        out_specs=jax.tree.map(lambda _: pl.BlockSpec(memory_space=place), out),
        scratch_shapes=scratch,
        input_output_aliases=aliases,
        compiler_params=pltpu.CompilerParams(vmem_limit_bytes=limit),
        cost_estimate=pl.CostEstimate(
            flops=2 * macs,
            bytes_accessed=sum(a.size * a.dtype.itemsize for a in list(args) + list(out)),
            transcendentals=0,
        ),
    )(*args)


def hold_kernel(src_ref, dst_ref):
    pass


def hold(value):
    return call(hold_kernel, (value,), (value,), 10**10, hbm=True, aliases={0: 0})[0]


def exchange(blocks, axes):
    return lax.all_to_all(blocks, axes, split_axis=0, concat_axis=0, tiled=True)


def softmax(values, axis):
    top = jnp.exp(values - jnp.max(values, axis=axis, keepdims=True))
    return top / jnp.sum(top, axis=axis, keepdims=True)


def route_kernel(tok, cot, par, out, dispatch_ref, combine_ref, pairs, sems):
    logits = dot(par[...], tok[...], ((1,), (1,)))
    dispatch = softmax(logits, 1)
    combine = softmax(logits, 0)
    pairs[:, 0, :] = dot(dispatch.astype(BF16), tok[...], ((1,), (0,))).astype(BF16)
    pairs[:, 1, :] = dot(combine.astype(BF16), cot[...], ((1,), (0,))).astype(BF16)
    copies = [pltpu.make_async_copy(pairs, out.at[y], sems.at[y]) for y in range(8)]
    for copy in copies:
        copy.start()
    dispatch_ref[...] = dispatch
    combine_ref[...] = combine
    for copy in copies:
        copy.wait()


def route(tokens, cotangent, params_t):
    hbm = pl.BlockSpec(memory_space=pl.ANY)
    vmem = pl.BlockSpec(memory_space=pltpu.VMEM)
    return pl.pallas_call(
        route_kernel,
        out_shape=(shape((8, 16, 2, 1408), BF16), shape((16, 256), F32), shape((16, 256), F32)),
        in_specs=[vmem, vmem, vmem],
        out_specs=(hbm, vmem, vmem),
        scratch_shapes=[pltpu.VMEM((16, 2, 1408), BF16), pltpu.SemaphoreType.DMA((8,))],
        compiler_params=pltpu.CompilerParams(vmem_limit_bytes=SMALL),
        cost_estimate=pl.CostEstimate(flops=4 * 10**7, bytes_accessed=3 * 10**6, transcendentals=0),
    )(tokens, cotangent, params_t)


def hidden_kernel(*refs):
    routed, weights, outs, scratch = refs[0], refs[1:9], refs[9:15], refs[15:]
    back_out, core_out, act_out, slope_out, x_out, g_out = outs
    rows, lifts, drops, x, g, act, slope, back, core, sems = scratch
    unpack = pltpu.make_async_copy(routed, rows, sems.at[0])
    unpack.start()
    order = (2, 3, 0, 1)
    loads = {}
    for k in order:
        part = pl.ds(192 * k, 192)
        loads[k] = (
            pltpu.make_async_copy(weights[2 * k], lifts.at[part], sems.at[1 + 2 * k]),
            pltpu.make_async_copy(weights[2 * k + 1], drops.at[part], sems.at[2 + 2 * k]),
        )
        for load in loads[k]:
            load.start()
    stores = []

    def store(src, dst):
        copy = pltpu.make_async_copy(src, dst, sems.at[9 + len(stores)])
        copy.start()
        stores.append(copy)

    unpack.wait()
    x[...] = rows[:, 0, :]
    g[...] = rows[:, 1, :]
    store(x, x_out)
    store(g, g_out)
    for k in order:
        part = pl.ds(192 * k, 192)
        for load in loads[k]:
            load.wait()
        preact = dot(lifts[part, :], x[...], ((1,), (1,)))
        activated_grad = dot(drops[part, :], g[...], ((1,), (1,)))
        rise = 0.5 * (1.0 + lax.erf(preact * 0.7071067811865476))
        bell = preact * jnp.exp(-0.5 * preact * preact) * 0.3989422804014327
        activated = (preact * rise).astype(BF16)
        preact_grad = (activated_grad * (rise + bell)).astype(BF16)
        act[part, :] = activated
        slope[part, :] = preact_grad
        if k >= 2:
            half = pl.ds(384 * (k - 2), 384)
            core[pl.ds(384 * (k - 2), 192), :] = dot(preact_grad, x[...], ((1,), (0,))).astype(BF16)
            core[pl.ds(384 * (k - 2) + 192, 192), :] = dot(
                activated, g[...], ((1,), (0,))
            ).astype(BF16)
            store(core.at[half], core_out.at[half])
    store(act, act_out)
    store(slope, slope_out)
    total = dot(slope[...], lifts[...], ((0,), (0,))).astype(BF16)
    back[:, 0, :] = total[:, :768]
    back[:, 1, :640] = total[:, 768:]
    back[:, 1, 640:] = jnp.zeros((128, 128), BF16)
    store(back, back_out)
    for copy in stores:
        copy.wait()


def block_grads(k, x_ref, g_ref, act_ref, slope_ref):
    rows = pl.ds(192 * k, 192)
    lift = dot(slope_ref[rows, :], x_ref[...], ((1,), (0,)))
    drop = dot(act_ref[rows, :], g_ref[...], ((1,), (0,)))
    return lift, drop


def x_kernel(x_ref, g_ref, act_ref, slope_ref, core_ref, out_ref):
    lift, drop = block_grads(1, x_ref, g_ref, act_ref, slope_ref)
    out_ref[:192, :] = (lift + core_ref[384:576, :].astype(F32)).astype(BF16)
    out_ref[192:, :] = (drop + core_ref[576:, :].astype(F32)).astype(BF16)


def own_kernel(x_ref, g_ref, act_ref, slope_ref, core_ref, over_ref, lift_ref, drop_ref):
    lift, drop = block_grads(0, x_ref, g_ref, act_ref, slope_ref)
    lift_ref[...] = (
        lift + core_ref[:192, :].astype(F32) + over_ref[:192, :].astype(F32)
    ).astype(BF16)
    drop_ref[...] = (
        drop + core_ref[192:384, :].astype(F32) + over_ref[192:, :].astype(F32)
    ).astype(BF16)


def combine_kernel(out_ref, cot, combine, grad_ref):
    grad = dot(out_ref[...], cot[...], ((1,), (1,)))
    weighted = jnp.sum(grad * combine[...], axis=0, keepdims=True)
    grad_ref[...] = combine[...] * (grad - weighted)


def image_kernel(returned, tok, par, dispatch, part, out, left_ref, right_ref):
    head = tail = None
    for y in range(8):
        rows = pl.ds(16 * y, 16)
        one = returned[rows, 0, :].astype(F32)
        two = returned[rows, 1, :].astype(F32)
        head = one if head is None else head + one
        tail = two if tail is None else tail + two
    slot_grad = jnp.concatenate([head, tail[:, :640]], axis=1).astype(BF16)
    right_ref[:16, :] = slot_grad
    right_ref[16:32, :] = par[...]
    right_ref[32:, :] = par[...]
    grad = dot(slot_grad, tok[...], ((1,), (1,)))
    weighted = jnp.sum(grad * dispatch[...], axis=1, keepdims=True)
    logit = part[...] + dispatch[...] * (grad - weighted)
    high = logit.astype(BF16)
    low = (logit - high.astype(F32)).astype(BF16)
    left_ref[:16, :] = dispatch[...].astype(BF16)
    left_ref[16:32, :] = high
    left_ref[32:, :] = low
    local = dot(high, tok[...], ((1,), (0,))) + dot(low, tok[...], ((1,), (0,)))
    local = local.astype(BF16)
    out[:, 0, :] = local[:, :768]
    out[:, 1, :640] = local[:, 768:]
    out[:, 1, 640:] = jnp.zeros((16, 128), BF16)


def shards(tokens, cotangent, slot_outputs, slot_params, lift_weight, drop_weight):
    tokens, cotangent, slot_outputs = tokens[0], cotangent[0], slot_outputs[0]
    lift, drop = lift_weight[0], drop_weight[0]
    x_lift = hold(lax.ppermute(lift, "xhi", SWAP))
    x_drop = hold(lax.ppermute(drop, "xhi", SWAP))
    x_lift, lift_later, drop_later = lax.optimization_barrier((x_lift, lift, drop))
    c_lift = lax.ppermute(lift_later, "core", SWAP)
    c_drop = lax.ppermute(drop_later, "core", SWAP)
    b_lift = lax.ppermute(x_lift, "core", SWAP)
    b_drop = lax.ppermute(x_drop, "core", SWAP)

    params_t = slot_params.T
    sent, dispatch, combine = route(tokens, cotangent, params_t)
    routed = exchange(sent.reshape(128, 2, 1408), HIDDEN)
    combine_part = call(
        combine_kernel,
        (shape((16, 256), F32),),
        (slot_outputs, cotangent, combine),
        16 * 256 * 1408,
    )[0]

    units = shape((768, 128), BF16)
    images = shape((128, 1408), BF16)
    core_half = shape((768, 1408), BF16)
    folded = shape((128, 2, 768), BF16)
    backward, to_core, activated, slopes, inputs, upstream = call(
        hidden_kernel,
        (folded, core_half, units, units, images, images),
        (routed, lift, drop, x_lift, x_drop, c_lift, c_drop, b_lift, b_drop),
        5 * 128 * 768 * 1408,
        hbm=True,
        scratch=[
            pltpu.VMEM(a.shape, BF16)
            for a in (
                routed, core_half, core_half, images, images, units, units, folded, core_half
            )
        ]
        + [pltpu.SemaphoreType.DMA((16,))],
    )
    returned = exchange(backward, HIDDEN)
    rows = (inputs, upstream, activated, slopes)
    from_core = lax.ppermute(to_core, "core", SWAP)
    to_x = call(
        x_kernel, (shape((384, 1408), BF16),), rows + (from_core,), 2 * 192 * 128 * 1408
    )[0]
    from_x = lax.ppermute(to_x, "xhi", SWAP)
    returned, to_x = lax.optimization_barrier((returned, to_x))
    half = shape((192, 1408), BF16)
    lift_grad, drop_grad = call(
        own_kernel, (half, half), rows + (from_core, from_x), 2 * 192 * 128 * 1408
    )

    local, left, right = call(
        image_kernel,
        (shape((16, 2, 768), BF16), shape((48, 256), BF16), shape((48, 1408), BF16)),
        (returned, tokens, params_t, dispatch, combine_part),
        3 * 16 * 256 * 1408,
        limit=SMALL,
    )
    by_slot = exchange(local, NEAR)
    by_slot = jnp.sum(by_slot.astype(F32), axis=0).astype(BF16)
    by_group = exchange(jnp.broadcast_to(by_slot[None], (32, 2, 768)), FAR)
    total = jnp.sum(by_group.astype(F32), axis=0).astype(BF16)
    columns = exchange(jnp.broadcast_to(total[None], (16, 2, 768)), NEAR)
    columns, lift_grad, drop_grad = lax.optimization_barrier((columns, lift_grad, drop_grad))
    param_grad = jnp.concatenate([columns[:, 0, :], columns[:, 1, :640]], axis=1).astype(F32).T

    token_grad = jnp.einsum("kp,kd->pd", left, right, preferred_element_type=F32).astype(BF16)
    return (token_grad[None], param_grad, lift_grad[None], drop_grad[None])


def solution(mesh):
    split = Mesh(mesh.devices.reshape(2, 8, 2, 8, 2), AXES)
    images = P(AXES, None, None)
    hidden = P(EXPERT, DP, None)
    return jax.shard_map(
        shards,
        mesh=split,
        in_specs=(images, images, images, P(), hidden, hidden),
        out_specs=(images, P(), hidden, hidden),
        check_vma=False,
    )
```

```python
import jax
import jax.numpy as jnp
from jax import lax
from jax.experimental import pallas as pl
from jax.experimental.pallas import tpu as pltpu
from jax.sharding import Mesh, PartitionSpec as P

AXES = ("xhi", "y", "core", "z", "xlo")
DP = ("xhi", "y", "core")
NEAR = ("core", "z")
FAR = ("xhi", "y", "xlo")
EXPERT = ("z", "xlo")
HIDDEN = ("y", "z", "xlo")
SWAP = [(0, 1), (1, 0)]
BF16 = jnp.bfloat16
F32 = jnp.float32
LIMIT = 56 * 2**20
SMALL = 24 * 2**20
shape = jax.ShapeDtypeStruct


def dot(a, b, contract):
    return lax.dot_general(a, b, (contract, ((), ())), preferred_element_type=F32)


def call(kernel, out, args, macs, hbm=False, scratch=(), aliases={}, limit=LIMIT):
    place = pl.ANY if hbm else pltpu.VMEM
    return pl.pallas_call(
        kernel,
        out_shape=out,
        in_specs=[pl.BlockSpec(memory_space=place) for a in args],
        out_specs=jax.tree.map(lambda _: pl.BlockSpec(memory_space=place), out),
        scratch_shapes=scratch,
        input_output_aliases=aliases,
        compiler_params=pltpu.CompilerParams(vmem_limit_bytes=limit),
        cost_estimate=pl.CostEstimate(
            flops=2 * macs,
            bytes_accessed=sum(a.size * a.dtype.itemsize for a in list(args) + list(out)),
            transcendentals=0,
        ),
    )(*args)


def hold_kernel(src_ref, dst_ref):
    pass


def hold(value):
    return call(
        hold_kernel, (value,), (value,), 10**10, hbm=True, aliases={0: 0}, limit=SMALL
    )[0]


def exchange(blocks, axes):
    return lax.all_to_all(blocks, axes, split_axis=0, concat_axis=0, tiled=True)


def softmax(values, axis):
    top = jnp.exp(values - jnp.max(values, axis=axis, keepdims=True))
    return top / jnp.sum(top, axis=axis, keepdims=True)


def route_kernel(tok, cot, par, out, dispatch_ref, combine_ref, pairs, sems):
    logits = dot(par[...], tok[...], ((1,), (1,)))
    dispatch = softmax(logits, 1)
    combine = softmax(logits, 0)
    pairs[:, 0, :] = dot(dispatch.astype(BF16), tok[...], ((1,), (0,))).astype(BF16)
    pairs[:, 1, :] = dot(combine.astype(BF16), cot[...], ((1,), (0,))).astype(BF16)
    copies = [pltpu.make_async_copy(pairs, out.at[y], sems.at[y]) for y in range(8)]
    for copy in copies:
        copy.start()
    dispatch_ref[...] = dispatch
    combine_ref[...] = combine
    for copy in copies:
        copy.wait()


def route(tokens, cotangent, params_t):
    hbm = pl.BlockSpec(memory_space=pl.ANY)
    vmem = pl.BlockSpec(memory_space=pltpu.VMEM)
    return pl.pallas_call(
        route_kernel,
        out_shape=(shape((8, 16, 2, 1408), BF16), shape((16, 256), F32), shape((16, 256), F32)),
        in_specs=[vmem, vmem, vmem],
        out_specs=(hbm, vmem, vmem),
        scratch_shapes=[pltpu.VMEM((16, 2, 1408), BF16), pltpu.SemaphoreType.DMA((8,))],
        compiler_params=pltpu.CompilerParams(vmem_limit_bytes=SMALL),
        cost_estimate=pl.CostEstimate(flops=4 * 10**7, bytes_accessed=3 * 10**6, transcendentals=0),
    )(tokens, cotangent, params_t)


def hidden_kernel(*refs):
    routed, weights, outs, scratch = refs[0], refs[1:5], refs[5:11], refs[11:]
    back_out, core_out, act_out, slope_out, x_out, g_out = outs
    rows, lifts, drops, x, g, act, slope, back, core, sems = scratch
    unpack = pltpu.make_async_copy(routed, rows, sems.at[0])
    unpack.start()
    order = (2, 3, 0, 1)
    loads = {}
    for k in order:
        part = pl.ds(192 * k, 192)
        loads[k] = (
            pltpu.make_async_copy(weights[k].at[pl.ds(0, 192)], lifts.at[part], sems.at[1 + 2 * k]),
            pltpu.make_async_copy(weights[k].at[pl.ds(192, 192)], drops.at[part], sems.at[2 + 2 * k]),
        )
        for load in loads[k]:
            load.start()
    stores = []

    def store(src, dst):
        copy = pltpu.make_async_copy(src, dst, sems.at[9 + len(stores)])
        copy.start()
        stores.append(copy)

    unpack.wait()
    for column in range(0, 1408, 128):
        lanes = pl.ds(column, 128)
        both = rows[:, :, lanes].astype(F32)
        x[:, lanes] = both[:, 0, :].astype(BF16)
        g[:, lanes] = both[:, 1, :].astype(BF16)
    store(x, x_out)
    store(g, g_out)
    for k in order:
        part = pl.ds(192 * k, 192)
        for load in loads[k]:
            load.wait()
        preact = dot(lifts[part, :], x[...], ((1,), (1,)))
        activated_grad = dot(drops[part, :], g[...], ((1,), (1,)))
        rise = 0.5 * (1.0 + lax.erf(preact * 0.7071067811865476))
        bell = preact * jnp.exp(-0.5 * preact * preact) * 0.3989422804014327
        activated = (preact * rise).astype(BF16)
        preact_grad = (activated_grad * (rise + bell)).astype(BF16)
        act[part, :] = activated
        slope[part, :] = preact_grad
        if k >= 2:
            half = pl.ds(384 * (k - 2), 384)
            core[pl.ds(384 * (k - 2), 192), :] = dot(preact_grad, x[...], ((1,), (0,))).astype(BF16)
            core[pl.ds(384 * (k - 2) + 192, 192), :] = dot(
                activated, g[...], ((1,), (0,))
            ).astype(BF16)
            store(core.at[half], core_out.at[half])
    store(act, act_out)
    store(slope, slope_out)
    total = dot(slope[...], lifts[...], ((0,), (0,))).astype(BF16)
    back[:, 0, :] = total[:, :768]
    back[:, 1, :640] = total[:, 768:]
    back[:, 1, 640:] = jnp.zeros((128, 128), BF16)
    store(back, back_out)
    for copy in stores:
        copy.wait()


def block_grads(k, x_ref, g_ref, act_ref, slope_ref):
    rows = pl.ds(192 * k, 192)
    lift = dot(slope_ref[rows, :], x_ref[...], ((1,), (0,)))
    drop = dot(act_ref[rows, :], g_ref[...], ((1,), (0,)))
    return lift, drop


def x_kernel(x_ref, g_ref, act_ref, slope_ref, core_ref, out_ref):
    lift, drop = block_grads(1, x_ref, g_ref, act_ref, slope_ref)
    out_ref[:192, :] = (lift + core_ref[384:576, :].astype(F32)).astype(BF16)
    out_ref[192:, :] = (drop + core_ref[576:, :].astype(F32)).astype(BF16)


def own_kernel(x_ref, g_ref, act_ref, slope_ref, core_ref, over_ref, lift_ref, drop_ref):
    lift, drop = block_grads(0, x_ref, g_ref, act_ref, slope_ref)
    lift_ref[...] = (
        lift + core_ref[:192, :].astype(F32) + over_ref[:192, :].astype(F32)
    ).astype(BF16)
    drop_ref[...] = (
        drop + core_ref[192:384, :].astype(F32) + over_ref[192:, :].astype(F32)
    ).astype(BF16)


def combine_kernel(out_ref, cot, combine, grad_ref):
    grad = dot(out_ref[...], cot[...], ((1,), (1,)))
    weighted = jnp.sum(grad * combine[...], axis=0, keepdims=True)
    grad_ref[...] = combine[...] * (grad - weighted)


def image_kernel(returned, tok, par, dispatch, part, out, left_ref, right_ref):
    head = tail = None
    for y in range(8):
        rows = pl.ds(16 * y, 16)
        one = returned[rows, 0, :].astype(F32)
        two = returned[rows, 1, :].astype(F32)
        head = one if head is None else head + one
        tail = two if tail is None else tail + two
    slot_grad = jnp.concatenate([head, tail[:, :640]], axis=1).astype(BF16)
    right_ref[:16, :] = slot_grad
    right_ref[16:32, :] = par[...]
    right_ref[32:, :] = par[...]
    grad = dot(slot_grad, tok[...], ((1,), (1,)))
    weighted = jnp.sum(grad * dispatch[...], axis=1, keepdims=True)
    logit = part[...] + dispatch[...] * (grad - weighted)
    high = logit.astype(BF16)
    low = (logit - high.astype(F32)).astype(BF16)
    left_ref[:16, :] = dispatch[...].astype(BF16)
    left_ref[16:32, :] = high
    left_ref[32:, :] = low
    local = dot(high, tok[...], ((1,), (0,))) + dot(low, tok[...], ((1,), (0,)))
    local = local.astype(BF16)
    out[:, 0, :] = local[:, :768]
    out[:, 1, :640] = local[:, 768:]
    out[:, 1, 640:] = jnp.zeros((16, 128), BF16)


def shards(tokens, cotangent, slot_outputs, slot_params, lift_weight, drop_weight):
    tokens, cotangent, slot_outputs = tokens[0], cotangent[0], slot_outputs[0]
    lift, drop = lift_weight[0], drop_weight[0]
    own = jnp.concatenate([lift, drop], axis=0)
    over_x = hold(lax.ppermute(own, "xhi", SWAP))
    over_x, own_later = lax.optimization_barrier((over_x, own))
    over_core = lax.ppermute(own_later, "core", SWAP)
    over_both = lax.ppermute(over_x, "core", SWAP)

    params_t = slot_params.T
    sent, dispatch, combine = route(tokens, cotangent, params_t)
    routed = exchange(sent.reshape(128, 2, 1408), HIDDEN)
    combine_part = call(
        combine_kernel,
        (shape((16, 256), F32),),
        (slot_outputs, cotangent, combine),
        16 * 256 * 1408,
    )[0]

    units = shape((768, 128), BF16)
    images = shape((128, 1408), BF16)
    core_half = shape((768, 1408), BF16)
    folded = shape((128, 2, 768), BF16)
    backward, to_core, activated, slopes, inputs, upstream = call(
        hidden_kernel,
        (folded, core_half, units, units, images, images),
        (routed, own, over_x, over_core, over_both),
        5 * 128 * 768 * 1408,
        hbm=True,
        scratch=[
            pltpu.VMEM(a.shape, BF16)
            for a in (
                routed, core_half, core_half, images, images, units, units, folded, core_half
            )
        ]
        + [pltpu.SemaphoreType.DMA((16,))],
    )
    returned = exchange(backward, HIDDEN)
    rows = (inputs, upstream, activated, slopes)
    from_core = lax.ppermute(to_core, "core", SWAP)
    to_x = call(
        x_kernel,
        (shape((384, 1408), BF16),),
        rows + (from_core,),
        2 * 192 * 128 * 1408,
        limit=SMALL,
    )[0]
    from_x = lax.ppermute(to_x, "xhi", SWAP)
    returned, to_x = lax.optimization_barrier((returned, to_x))
    half = shape((192, 1408), BF16)
    lift_grad, drop_grad = call(
        own_kernel,
        (half, half),
        rows + (from_core, from_x),
        2 * 192 * 128 * 1408,
        limit=SMALL,
    )

    local, left, right = call(
        image_kernel,
        (shape((16, 2, 768), BF16), shape((48, 256), BF16), shape((48, 1408), BF16)),
        (returned, tokens, params_t, dispatch, combine_part),
        3 * 16 * 256 * 1408,
        limit=SMALL,
    )
    by_slot = exchange(local, NEAR)
    by_slot = jnp.sum(by_slot.astype(F32), axis=0).astype(BF16)
    by_group = exchange(jnp.broadcast_to(by_slot[None], (32, 2, 768)), FAR)
    total = jnp.sum(by_group.astype(F32), axis=0).astype(BF16)
    columns = exchange(jnp.broadcast_to(total[None], (16, 2, 768)), NEAR)
    columns, lift_grad, drop_grad = lax.optimization_barrier((columns, lift_grad, drop_grad))
    param_grad = jnp.concatenate([columns[:, 0, :], columns[:, 1, :640]], axis=1).astype(F32).T

    token_grad = jnp.einsum("kp,kd->pd", left, right, preferred_element_type=F32).astype(BF16)
    return (token_grad[None], param_grad, lift_grad[None], drop_grad[None])


def solution(mesh):
    split = Mesh(mesh.devices.reshape(2, 8, 2, 8, 2), AXES)
    images = P(AXES, None, None)
    hidden = P(EXPERT, DP, None)
    return jax.shard_map(
        shards,
        mesh=split,
        in_specs=(images, images, images, P(), hidden, hidden),
        out_specs=(images, P(), hidden, hidden),
        check_vma=False,
    )
```

```python
import jax
import jax.numpy as jnp
from jax import lax
from jax.experimental import pallas as pl
from jax.experimental.pallas import tpu as pltpu
from jax.sharding import Mesh, PartitionSpec as P

AXES = ("xhi", "y", "core", "z", "xlo")
DP = ("xhi", "y", "core")
NEAR = ("core", "z")
FAR = ("xhi", "y", "xlo")
EXPERT = ("z", "xlo")
HIDDEN = ("y", "z", "xlo")
SWAP = [(0, 1), (1, 0)]
BF16 = jnp.bfloat16
F32 = jnp.float32
LIMIT = 56 * 2**20
SMALL = 24 * 2**20
shape = jax.ShapeDtypeStruct


def dot(a, b, contract):
    return lax.dot_general(a, b, (contract, ((), ())), preferred_element_type=F32)


def call(kernel, out, args, macs, hbm=False, scratch=(), aliases={}, limit=LIMIT, out_place=None):
    place = pl.ANY if hbm else pltpu.VMEM
    return pl.pallas_call(
        kernel,
        out_shape=out,
        in_specs=[pl.BlockSpec(memory_space=place) for a in args],
        out_specs=jax.tree.map(lambda _: out_place or pl.BlockSpec(memory_space=place), out),
        scratch_shapes=scratch,
        input_output_aliases=aliases,
        compiler_params=pltpu.CompilerParams(vmem_limit_bytes=limit),
        cost_estimate=pl.CostEstimate(
            flops=2 * macs,
            bytes_accessed=sum(a.size * a.dtype.itemsize for a in list(args) + list(out)),
            transcendentals=0,
        ),
    )(*args)


def hold_kernel(src_ref, dst_ref):
    pass


def hold(value):
    return call(
        hold_kernel, (value,), (value,), 10**10, hbm=True, aliases={0: 0}, limit=SMALL
    )[0]


def exchange(blocks, axes):
    return lax.all_to_all(blocks, axes, split_axis=0, concat_axis=0, tiled=True)


def softmax(values, axis):
    top = jnp.exp(values - jnp.max(values, axis=axis, keepdims=True))
    return top / jnp.sum(top, axis=axis, keepdims=True)


def route_kernel(tok, cot, par, out, dispatch_ref, combine_ref, pairs, sems):
    logits = dot(par[...], tok[...], ((1,), (1,)))
    dispatch = softmax(logits, 1)
    combine = softmax(logits, 0)
    pairs[:, 0, :] = dot(dispatch.astype(BF16), tok[...], ((1,), (0,))).astype(BF16)
    pairs[:, 1, :] = dot(combine.astype(BF16), cot[...], ((1,), (0,))).astype(BF16)
    copies = [pltpu.make_async_copy(pairs, out.at[y], sems.at[y]) for y in range(8)]
    for copy in copies:
        copy.start()
    dispatch_ref[...] = dispatch
    combine_ref[...] = combine
    for copy in copies:
        copy.wait()


def route(tokens, cotangent, params_t):
    hbm = pl.BlockSpec(memory_space=pl.ANY)
    vmem = pl.BlockSpec(memory_space=pltpu.VMEM)
    return pl.pallas_call(
        route_kernel,
        out_shape=(shape((8, 16, 2, 1408), BF16), shape((16, 256), F32), shape((16, 256), F32)),
        in_specs=[vmem, vmem, vmem],
        out_specs=(hbm, vmem, vmem),
        scratch_shapes=[pltpu.VMEM((16, 2, 1408), BF16), pltpu.SemaphoreType.DMA((8,))],
        compiler_params=pltpu.CompilerParams(vmem_limit_bytes=SMALL),
        cost_estimate=pl.CostEstimate(flops=4 * 10**7, bytes_accessed=3 * 10**6, transcendentals=0),
    )(tokens, cotangent, params_t)


def hidden_kernel(*refs):
    routed, weights, outs, scratch = refs[0], refs[1:5], refs[5:11], refs[11:]
    back_out, core_out, act_out, slope_out, x_out, g_out = outs
    rows, lifts, drops, x, g, act, slope, back, core, sems = scratch
    unpack = pltpu.make_async_copy(routed, rows, sems.at[0])
    unpack.start()
    order = (2, 3, 0, 1)
    loads = {}
    for k in order:
        part = pl.ds(192 * k, 192)
        loads[k] = (
            pltpu.make_async_copy(weights[k].at[pl.ds(0, 192)], lifts.at[part], sems.at[1 + 2 * k]),
            pltpu.make_async_copy(weights[k].at[pl.ds(192, 192)], drops.at[part], sems.at[2 + 2 * k]),
        )
        for load in loads[k]:
            load.start()
    stores = []

    def store(src, dst):
        copy = pltpu.make_async_copy(src, dst, sems.at[9 + len(stores)])
        copy.start()
        stores.append(copy)

    unpack.wait()
    for column in range(0, 1408, 128):
        lanes = pl.ds(column, 128)
        both = rows[:, :, lanes].astype(F32)
        x[:, lanes] = both[:, 0, :].astype(BF16)
        g[:, lanes] = both[:, 1, :].astype(BF16)
    store(x, x_out)
    store(g, g_out)
    for k in order:
        part = pl.ds(192 * k, 192)
        for load in loads[k]:
            load.wait()
        preact = dot(lifts[part, :], x[...], ((1,), (1,)))
        activated_grad = dot(drops[part, :], g[...], ((1,), (1,)))
        rise = 0.5 * (1.0 + lax.erf(preact * 0.7071067811865476))
        bell = preact * jnp.exp(-0.5 * preact * preact) * 0.3989422804014327
        activated = (preact * rise).astype(BF16)
        preact_grad = (activated_grad * (rise + bell)).astype(BF16)
        act[part, :] = activated
        slope[part, :] = preact_grad
        if k >= 2:
            half = pl.ds(384 * (k - 2), 384)
            core[pl.ds(384 * (k - 2), 192), :] = dot(preact_grad, x[...], ((1,), (0,))).astype(BF16)
            core[pl.ds(384 * (k - 2) + 192, 192), :] = dot(
                activated, g[...], ((1,), (0,))
            ).astype(BF16)
            store(core.at[half], core_out.at[half])
    store(act, act_out)
    store(slope, slope_out)
    total = dot(slope[...], lifts[...], ((0,), (0,))).astype(BF16)
    back[:, 0, :] = total[:, :768]
    back[:, 1, :640] = total[:, 768:]
    back[:, 1, 640:] = jnp.zeros((128, 128), BF16)
    store(back, back_out)
    for copy in stores:
        copy.wait()


def fetch(pairs, sems):
    copies = [pltpu.make_async_copy(a, b, sems.at[k]) for k, (a, b) in enumerate(pairs)]
    for copy in copies:
        copy.start()
    return copies


def x_kernel(x_in, g_in, act_in, slope_in, core_in, out_ref, x, g, act, slope, core, sems):
    rows = pl.ds(192, 192)
    copies = fetch(
        (
            (slope_in.at[rows], slope),
            (x_in, x),
            (act_in.at[rows], act),
            (g_in, g),
            (core_in.at[pl.ds(384, 384)], core),
        ),
        sems,
    )
    copies[0].wait()
    copies[1].wait()
    lift = dot(slope[...], x[...], ((1,), (0,)))
    copies[2].wait()
    copies[3].wait()
    drop = dot(act[...], g[...], ((1,), (0,)))
    copies[4].wait()
    out_ref[:192, :] = (lift + core[:192, :].astype(F32)).astype(BF16)
    out_ref[192:, :] = (drop + core[192:, :].astype(F32)).astype(BF16)


def own_kernel(
    x_in, g_in, act_in, slope_in, core_in, over_in, lift_ref, drop_ref,
    x, g, act, slope, core, over, sems,
):
    rows = pl.ds(0, 192)
    copies = fetch(
        (
            (slope_in.at[rows], slope),
            (x_in, x),
            (act_in.at[rows], act),
            (g_in, g),
            (core_in.at[pl.ds(0, 384)], core),
            (over_in, over),
        ),
        sems,
    )
    copies[0].wait()
    copies[1].wait()
    lift = dot(slope[...], x[...], ((1,), (0,)))
    copies[2].wait()
    copies[3].wait()
    drop = dot(act[...], g[...], ((1,), (0,)))
    copies[4].wait()
    copies[5].wait()
    lift_ref[...] = (lift + core[:192, :].astype(F32) + over[:192, :].astype(F32)).astype(BF16)
    drop_ref[...] = (drop + core[192:, :].astype(F32) + over[192:, :].astype(F32)).astype(BF16)


def combine_kernel(out_ref, cot, combine, grad_ref):
    grad = dot(out_ref[...], cot[...], ((1,), (1,)))
    weighted = jnp.sum(grad * combine[...], axis=0, keepdims=True)
    grad_ref[...] = combine[...] * (grad - weighted)


def image_kernel(
    returned, tok, par, dispatch_in, part_in, out, left_ref, right_ref, dispatch, part, sems
):
    loads = fetch(((dispatch_in, dispatch), (part_in, part)), sems)
    head = tail = None
    for y in range(8):
        rows = pl.ds(16 * y, 16)
        one = returned[rows, 0, :].astype(F32)
        two = returned[rows, 1, :].astype(F32)
        head = one if head is None else head + one
        tail = two if tail is None else tail + two
    slot_grad = jnp.concatenate([head, tail[:, :640]], axis=1).astype(BF16)
    right_ref[:16, :] = slot_grad
    right_ref[16:32, :] = par[...]
    right_ref[32:, :] = par[...]
    grad = dot(slot_grad, tok[...], ((1,), (1,)))
    for load in loads:
        load.wait()
    weighted = jnp.sum(grad * dispatch[...], axis=1, keepdims=True)
    logit = part[...] + dispatch[...] * (grad - weighted)
    high = logit.astype(BF16)
    low = (logit - high.astype(F32)).astype(BF16)
    left_ref[:16, :] = dispatch[...].astype(BF16)
    left_ref[16:32, :] = high
    left_ref[32:, :] = low
    local = dot(high, tok[...], ((1,), (0,))) + dot(low, tok[...], ((1,), (0,)))
    local = local.astype(BF16)
    out[:, 0, :] = local[:, :768]
    out[:, 1, :640] = local[:, 768:]
    out[:, 1, 640:] = jnp.zeros((16, 128), BF16)


def shards(tokens, cotangent, slot_outputs, slot_params, lift_weight, drop_weight):
    tokens, cotangent, slot_outputs = tokens[0], cotangent[0], slot_outputs[0]
    lift, drop = lift_weight[0], drop_weight[0]
    own = jnp.concatenate([lift, drop], axis=0)
    over_x = hold(lax.ppermute(own, "xhi", SWAP))
    over_both = lax.ppermute(over_x, "core", SWAP)

    params_t = slot_params.T
    sent, dispatch, combine = route(tokens, cotangent, params_t)
    combine, own_later = lax.optimization_barrier((combine, own))
    over_core = lax.ppermute(own_later, "core", SWAP)
    routed = exchange(sent.reshape(128, 2, 1408), HIDDEN)
    combine_part = call(
        combine_kernel,
        (shape((16, 256), F32),),
        (slot_outputs, cotangent, combine),
        16 * 256 * 1408,
    )[0]

    units = shape((768, 128), BF16)
    images = shape((128, 1408), BF16)
    core_half = shape((768, 1408), BF16)
    folded = shape((128, 2, 768), BF16)
    backward, to_core, activated, slopes, inputs, upstream = call(
        hidden_kernel,
        (folded, core_half, units, units, images, images),
        (routed, own, over_x, over_core, over_both),
        5 * 128 * 768 * 1408,
        hbm=True,
        scratch=[
            pltpu.VMEM(a.shape, BF16)
            for a in (
                routed, core_half, core_half, images, images, units, units, folded, core_half
            )
        ]
        + [pltpu.SemaphoreType.DMA((16,))],
    )
    returned = exchange(backward, HIDDEN)
    rows = (inputs, upstream, activated, slopes)
    from_core = lax.ppermute(to_core, "core", SWAP)
    vmem = pl.BlockSpec(memory_space=pltpu.VMEM)
    quarter = [
        pltpu.VMEM(size, BF16) for size in ((128, 1408),) * 2 + ((192, 128),) * 2 + ((384, 1408),)
    ]
    to_x = call(
        x_kernel,
        (shape((384, 1408), BF16),),
        rows + (from_core,),
        2 * 192 * 128 * 1408,
        hbm=True,
        out_place=vmem,
        scratch=quarter + [pltpu.SemaphoreType.DMA((5,))],
    )[0]
    from_x = lax.ppermute(to_x, "xhi", SWAP)
    returned, to_x = lax.optimization_barrier((returned, to_x))
    half = shape((192, 1408), BF16)
    lift_grad, drop_grad = call(
        own_kernel,
        (half, half),
        rows + (from_core, from_x),
        2 * 192 * 128 * 1408,
        hbm=True,
        out_place=vmem,
        scratch=quarter + quarter[4:] + [pltpu.SemaphoreType.DMA((6,))],
    )

    local, left, right = pl.pallas_call(
        image_kernel,
        out_shape=(shape((16, 2, 768), BF16), shape((48, 256), BF16), shape((48, 1408), BF16)),
        in_specs=[vmem] * 3 + [pl.BlockSpec(memory_space=pl.ANY)] * 2,
        out_specs=(vmem,) * 3,
        scratch_shapes=[pltpu.VMEM((16, 256), F32)] * 2 + [pltpu.SemaphoreType.DMA((2,))],
        compiler_params=pltpu.CompilerParams(vmem_limit_bytes=SMALL),
        cost_estimate=pl.CostEstimate(flops=4 * 10**7, bytes_accessed=2 * 10**6, transcendentals=0),
    )(returned, tokens, params_t, dispatch, combine_part)
    by_slot = exchange(local, NEAR)
    by_slot = jnp.sum(by_slot.astype(F32), axis=0).astype(BF16)
    by_group = exchange(jnp.broadcast_to(by_slot[None], (32, 2, 768)), FAR)
    total = jnp.sum(by_group.astype(F32), axis=0).astype(BF16)
    columns = exchange(jnp.broadcast_to(total[None], (16, 2, 768)), NEAR)
    columns, lift_grad, drop_grad = lax.optimization_barrier((columns, lift_grad, drop_grad))
    param_grad = jnp.concatenate([columns[:, 0, :], columns[:, 1, :640]], axis=1).astype(F32).T

    token_grad = jnp.einsum("kp,kd->pd", left, right, preferred_element_type=F32).astype(BF16)
    return (token_grad[None], param_grad, lift_grad[None], drop_grad[None])


def solution(mesh):
    split = Mesh(mesh.devices.reshape(2, 8, 2, 8, 2), AXES)
    images = P(AXES, None, None)
    hidden = P(EXPERT, DP, None)
    return jax.shard_map(
        shards,
        mesh=split,
        in_specs=(images, images, images, P(), hidden, hidden),
        out_specs=(images, P(), hidden, hidden),
        check_vma=False,
    )
```

```python
import jax
import jax.numpy as jnp
from jax import lax
from jax.experimental import pallas as pl
from jax.experimental.pallas import tpu as pltpu
from jax.sharding import Mesh, PartitionSpec as P

AXES = ("xhi", "y", "core", "z", "xlo")
DP = ("xhi", "y", "core")
NEAR = ("core", "z")
FAR = ("xhi", "y", "xlo")
EXPERT = ("z", "xlo")
HIDDEN = ("y", "z", "xlo")
SWAP = [(0, 1), (1, 0)]
BF16 = jnp.bfloat16
F32 = jnp.float32
LIMIT = 56 * 2**20
SMALL = 24 * 2**20
shape = jax.ShapeDtypeStruct


def dot(a, b, contract):
    return lax.dot_general(a, b, (contract, ((), ())), preferred_element_type=F32)


def call(kernel, out, args, macs, hbm=False, scratch=(), aliases={}, limit=LIMIT, out_place=None):
    place = pl.ANY if hbm else pltpu.VMEM
    return pl.pallas_call(
        kernel,
        out_shape=out,
        in_specs=[pl.BlockSpec(memory_space=place) for a in args],
        out_specs=jax.tree.map(lambda _: out_place or pl.BlockSpec(memory_space=place), out),
        scratch_shapes=scratch,
        input_output_aliases=aliases,
        compiler_params=pltpu.CompilerParams(vmem_limit_bytes=limit),
        cost_estimate=pl.CostEstimate(
            flops=2 * macs,
            bytes_accessed=sum(a.size * a.dtype.itemsize for a in list(args) + list(out)),
            transcendentals=0,
        ),
    )(*args)


def hold_kernel(src_ref, dst_ref):
    pass


def hold(value):
    return call(
        hold_kernel, (value,), (value,), 10**10, hbm=True, aliases={0: 0}, limit=SMALL
    )[0]


def exchange(blocks, axes):
    return lax.all_to_all(blocks, axes, split_axis=0, concat_axis=0, tiled=True)


def softmax(values, axis):
    top = jnp.exp(values - jnp.max(values, axis=axis, keepdims=True))
    return top / jnp.sum(top, axis=axis, keepdims=True)


def route_kernel(tok, cot, par, out, dispatch_ref, combine_ref, pairs, sems):
    logits = dot(par[...], tok[...], ((1,), (1,)))
    dispatch = softmax(logits, 1)
    combine = softmax(logits, 0)
    pairs[:, 0, :] = dot(dispatch.astype(BF16), tok[...], ((1,), (0,))).astype(BF16)
    pairs[:, 1, :] = dot(combine.astype(BF16), cot[...], ((1,), (0,))).astype(BF16)
    copies = [pltpu.make_async_copy(pairs, out.at[y], sems.at[y]) for y in range(8)]
    for copy in copies:
        copy.start()
    dispatch_ref[...] = dispatch
    combine_ref[...] = combine
    for copy in copies:
        copy.wait()


def route(tokens, cotangent, params_t):
    hbm = pl.BlockSpec(memory_space=pl.ANY)
    vmem = pl.BlockSpec(memory_space=pltpu.VMEM)
    return pl.pallas_call(
        route_kernel,
        out_shape=(shape((8, 16, 2, 1408), BF16), shape((16, 256), F32), shape((16, 256), F32)),
        in_specs=[vmem, vmem, vmem],
        out_specs=(hbm, vmem, vmem),
        scratch_shapes=[pltpu.VMEM((16, 2, 1408), BF16), pltpu.SemaphoreType.DMA((8,))],
        compiler_params=pltpu.CompilerParams(vmem_limit_bytes=SMALL),
        cost_estimate=pl.CostEstimate(flops=4 * 10**7, bytes_accessed=3 * 10**6, transcendentals=0),
    )(tokens, cotangent, params_t)


def hidden_kernel(*refs):
    routed, weights, outs, scratch = refs[0], refs[1:5], refs[5:11], refs[11:]
    back_out, core_out, act_out, slope_out, x_out, g_out = outs
    rows, lifts, drops, x, g, act, slope, back, core, sems = scratch
    unpack = pltpu.make_async_copy(routed, rows, sems.at[0])
    unpack.start()
    order = (2, 3, 0, 1)
    loads = {}
    for k in order:
        part = pl.ds(192 * k, 192)
        loads[k] = (
            pltpu.make_async_copy(weights[k].at[pl.ds(0, 192)], lifts.at[part], sems.at[1 + 2 * k]),
            pltpu.make_async_copy(weights[k].at[pl.ds(192, 192)], drops.at[part], sems.at[2 + 2 * k]),
        )
        for load in loads[k]:
            load.start()
    stores = []

    def store(src, dst):
        copy = pltpu.make_async_copy(src, dst, sems.at[9 + len(stores)])
        copy.start()
        stores.append(copy)

    unpack.wait()
    for column in range(0, 1408, 128):
        lanes = pl.ds(column, 128)
        both = rows[:, :, lanes].astype(F32)
        x[:, lanes] = both[:, 0, :].astype(BF16)
        g[:, lanes] = both[:, 1, :].astype(BF16)
    store(x, x_out)
    store(g, g_out)
    for k in order:
        part = pl.ds(192 * k, 192)
        for load in loads[k]:
            load.wait()
        preact = dot(lifts[part, :], x[...], ((1,), (1,)))
        activated_grad = dot(drops[part, :], g[...], ((1,), (1,)))
        rise = 0.5 * (1.0 + lax.erf(preact * 0.7071067811865476))
        bell = preact * jnp.exp(-0.5 * preact * preact) * 0.3989422804014327
        activated = (preact * rise).astype(BF16)
        preact_grad = (activated_grad * (rise + bell)).astype(BF16)
        act[part, :] = activated
        slope[part, :] = preact_grad
        if k >= 2:
            half = pl.ds(384 * (k - 2), 384)
            core[pl.ds(384 * (k - 2), 192), :] = dot(preact_grad, x[...], ((1,), (0,))).astype(BF16)
            core[pl.ds(384 * (k - 2) + 192, 192), :] = dot(
                activated, g[...], ((1,), (0,))
            ).astype(BF16)
            store(core.at[half], core_out.at[half])
    store(act, act_out)
    store(slope, slope_out)
    total = dot(slope[...], lifts[...], ((0,), (0,))).astype(BF16)
    back[:, 0, :] = total[:, :768]
    back[:, 1, :640] = total[:, 768:]
    back[:, 1, 640:] = jnp.zeros((128, 128), BF16)
    store(back, back_out)
    for copy in stores:
        copy.wait()


def fetch(pairs, sems):
    copies = [pltpu.make_async_copy(a, b, sems.at[k]) for k, (a, b) in enumerate(pairs)]
    for copy in copies:
        copy.start()
    return copies


def x_kernel(x_in, g_in, act_in, slope_in, core_in, out_ref, x, g, act, slope, core, sems):
    rows = pl.ds(192, 192)
    copies = fetch(
        (
            (slope_in.at[rows], slope),
            (x_in, x),
            (act_in.at[rows], act),
            (g_in, g),
            (core_in.at[pl.ds(384, 384)], core),
        ),
        sems,
    )
    copies[0].wait()
    copies[1].wait()
    lift = dot(slope[...], x[...], ((1,), (0,)))
    copies[2].wait()
    copies[3].wait()
    drop = dot(act[...], g[...], ((1,), (0,)))
    copies[4].wait()
    out_ref[:192, :] = (lift + core[:192, :].astype(F32)).astype(BF16)
    out_ref[192:, :] = (drop + core[192:, :].astype(F32)).astype(BF16)


def own_kernel(
    x_in, g_in, act_in, slope_in, core_in, over_in, lift_ref, drop_ref,
    x, g, act, slope, core, over, sems,
):
    rows = pl.ds(0, 192)
    copies = fetch(
        (
            (slope_in.at[rows], slope),
            (x_in, x),
            (act_in.at[rows], act),
            (g_in, g),
            (core_in.at[pl.ds(0, 384)], core),
            (over_in, over),
        ),
        sems,
    )
    copies[0].wait()
    copies[1].wait()
    lift = dot(slope[...], x[...], ((1,), (0,)))
    copies[2].wait()
    copies[3].wait()
    drop = dot(act[...], g[...], ((1,), (0,)))
    copies[4].wait()
    copies[5].wait()
    lift_ref[...] = (lift + core[:192, :].astype(F32) + over[:192, :].astype(F32)).astype(BF16)
    drop_ref[...] = (drop + core[192:, :].astype(F32) + over[192:, :].astype(F32)).astype(BF16)


def combine_kernel(out_ref, cot, combine, grad_ref):
    grad = dot(out_ref[...], cot[...], ((1,), (1,)))
    weighted = jnp.sum(grad * combine[...], axis=0, keepdims=True)
    grad_ref[...] = combine[...] * (grad - weighted)


def image_kernel(
    returned, tok, par, dispatch_in, part_in, out, left_ref, right_ref, dispatch, part, sems
):
    loads = fetch(((dispatch_in, dispatch), (part_in, part)), sems)
    head = tail = None
    for y in range(8):
        rows = pl.ds(16 * y, 16)
        one = returned[rows, 0, :].astype(F32)
        two = returned[rows, 1, :].astype(F32)
        head = one if head is None else head + one
        tail = two if tail is None else tail + two
    slot_grad = jnp.concatenate([head, tail[:, :640]], axis=1).astype(BF16)
    right_ref[:16, :] = slot_grad
    right_ref[16:32, :] = par[...]
    right_ref[32:, :] = par[...]
    grad = dot(slot_grad, tok[...], ((1,), (1,)))
    for load in loads:
        load.wait()
    weighted = jnp.sum(grad * dispatch[...], axis=1, keepdims=True)
    logit = part[...] + dispatch[...] * (grad - weighted)
    high = logit.astype(BF16)
    low = (logit - high.astype(F32)).astype(BF16)
    left_ref[:16, :] = dispatch[...].astype(BF16)
    left_ref[16:32, :] = high
    left_ref[32:, :] = low
    local = dot(high, tok[...], ((1,), (0,))) + dot(low, tok[...], ((1,), (0,)))
    local = local.astype(BF16)
    out[:, 0, :] = local[:, :768]
    out[:, 1, :640] = local[:, 768:]
    out[:, 1, 640:] = jnp.zeros((16, 128), BF16)


def shards(tokens, cotangent, slot_outputs, slot_params, lift_weight, drop_weight):
    tokens, cotangent, slot_outputs = tokens[0], cotangent[0], slot_outputs[0]
    lift, drop = lift_weight[0], drop_weight[0]
    own = jnp.concatenate([lift, drop], axis=0)
    over_x = hold(lax.ppermute(own, "xhi", SWAP))
    over_both = lax.ppermute(over_x, "core", SWAP)

    params_t = slot_params.T
    sent, dispatch, combine = route(tokens, cotangent, params_t)
    combine, lift, drop = lax.optimization_barrier((combine, lift, drop))
    own = jnp.concatenate([lift, drop], axis=0)
    over_core = lax.ppermute(own, "core", SWAP)
    routed = exchange(sent.reshape(128, 2, 1408), HIDDEN)
    combine_part = call(
        combine_kernel,
        (shape((16, 256), F32),),
        (slot_outputs, cotangent, combine),
        16 * 256 * 1408,
    )[0]

    routed, combine_part = lax.optimization_barrier((routed, combine_part))
    units = shape((768, 128), BF16)
    images = shape((128, 1408), BF16)
    core_half = shape((768, 1408), BF16)
    folded = shape((128, 2, 768), BF16)
    backward, to_core, activated, slopes, inputs, upstream = call(
        hidden_kernel,
        (folded, core_half, units, units, images, images),
        (routed, own, over_x, over_core, over_both),
        5 * 128 * 768 * 1408,
        hbm=True,
        scratch=[
            pltpu.VMEM(a.shape, BF16)
            for a in (
                routed, core_half, core_half, images, images, units, units, folded, core_half
            )
        ]
        + [pltpu.SemaphoreType.DMA((16,))],
    )
    returned = exchange(backward, HIDDEN)
    rows = (inputs, upstream, activated, slopes)
    from_core = lax.ppermute(to_core, "core", SWAP)
    vmem = pl.BlockSpec(memory_space=pltpu.VMEM)
    quarter = [
        pltpu.VMEM(size, BF16) for size in ((128, 1408),) * 2 + ((192, 128),) * 2 + ((384, 1408),)
    ]
    to_x = call(
        x_kernel,
        (shape((384, 1408), BF16),),
        rows + (from_core,),
        2 * 192 * 128 * 1408,
        hbm=True,
        out_place=vmem,
        scratch=quarter + [pltpu.SemaphoreType.DMA((5,))],
    )[0]
    from_x = lax.ppermute(to_x, "xhi", SWAP)
    returned, to_x = lax.optimization_barrier((returned, to_x))
    half = shape((192, 1408), BF16)
    lift_grad, drop_grad = call(
        own_kernel,
        (half, half),
        rows + (from_core, from_x),
        2 * 192 * 128 * 1408,
        hbm=True,
        out_place=vmem,
        scratch=quarter + quarter[4:] + [pltpu.SemaphoreType.DMA((6,))],
    )

    local, left, right = pl.pallas_call(
        image_kernel,
        out_shape=(shape((16, 2, 768), BF16), shape((48, 256), BF16), shape((48, 1408), BF16)),
        in_specs=[vmem] * 3 + [pl.BlockSpec(memory_space=pl.ANY)] * 2,
        out_specs=(vmem,) * 3,
        scratch_shapes=[pltpu.VMEM((16, 256), F32)] * 2 + [pltpu.SemaphoreType.DMA((2,))],
        compiler_params=pltpu.CompilerParams(vmem_limit_bytes=SMALL),
        cost_estimate=pl.CostEstimate(flops=4 * 10**7, bytes_accessed=2 * 10**6, transcendentals=0),
    )(returned, tokens, params_t, dispatch, combine_part)
    by_slot = exchange(local, NEAR)
    by_slot = jnp.sum(by_slot.astype(F32), axis=0).astype(BF16)
    by_group = exchange(jnp.broadcast_to(by_slot[None], (32, 2, 768)), FAR)
    total = jnp.sum(by_group.astype(F32), axis=0).astype(BF16)
    columns = exchange(jnp.broadcast_to(total[None], (16, 2, 768)), NEAR)
    columns, lift_grad, drop_grad = lax.optimization_barrier((columns, lift_grad, drop_grad))
    param_grad = jnp.concatenate([columns[:, 0, :], columns[:, 1, :640]], axis=1).astype(F32).T

    token_grad = jnp.einsum("kp,kd->pd", left, right, preferred_element_type=F32).astype(BF16)
    return (token_grad[None], param_grad, lift_grad[None], drop_grad[None])


def solution(mesh):
    split = Mesh(mesh.devices.reshape(2, 8, 2, 8, 2), AXES)
    images = P(AXES, None, None)
    hidden = P(EXPERT, DP, None)
    return jax.shard_map(
        shards,
        mesh=split,
        in_specs=(images, images, images, P(), hidden, hidden),
        out_specs=(images, P(), hidden, hidden),
        check_vma=False,
    )
```

```python
import jax
import jax.numpy as jnp
from jax import lax
from jax.experimental import pallas as pl
from jax.experimental.pallas import tpu as pltpu
from jax.sharding import Mesh, PartitionSpec as P

AXES = ("xhi", "y", "core", "z", "xlo")
DP = ("xhi", "y", "core")
NEAR = ("core", "z")
FAR = ("xhi", "y", "xlo")
EXPERT = ("z", "xlo")
HIDDEN = ("y", "z", "xlo")
SWAP = [(0, 1), (1, 0)]
BF16 = jnp.bfloat16
F32 = jnp.float32
LIMIT = 56 * 2**20
SMALL = 24 * 2**20
shape = jax.ShapeDtypeStruct


def dot(a, b, contract):
    return lax.dot_general(a, b, (contract, ((), ())), preferred_element_type=F32)


def call(kernel, out, args, macs, hbm=False, scratch=(), aliases={}, limit=LIMIT, out_place=None):
    place = pl.ANY if hbm else pltpu.VMEM
    return pl.pallas_call(
        kernel,
        out_shape=out,
        in_specs=[pl.BlockSpec(memory_space=place) for a in args],
        out_specs=jax.tree.map(lambda _: out_place or pl.BlockSpec(memory_space=place), out),
        scratch_shapes=scratch,
        input_output_aliases=aliases,
        compiler_params=pltpu.CompilerParams(vmem_limit_bytes=limit),
        cost_estimate=pl.CostEstimate(
            flops=2 * macs,
            bytes_accessed=sum(a.size * a.dtype.itemsize for a in list(args) + list(out)),
            transcendentals=0,
        ),
    )(*args)


def join_kernel(lift, drop, out, sems):
    copies = fetch(
        ((lift, out.at[pl.ds(0, 192)]), (drop, out.at[pl.ds(192, 192)])), sems
    )
    for copy in copies:
        copy.wait()


def hold_kernel(src_ref, dst_ref):
    pass


def hold(value):
    return call(
        hold_kernel, (value,), (value,), 10**10, hbm=True, aliases={0: 0}, limit=SMALL
    )[0]


def exchange(blocks, axes):
    return lax.all_to_all(blocks, axes, split_axis=0, concat_axis=0, tiled=True)


def softmax(values, axis):
    top = jnp.exp(values - jnp.max(values, axis=axis, keepdims=True))
    return top / jnp.sum(top, axis=axis, keepdims=True)


def route_kernel(tok, cot, par, out, dispatch_ref, combine_ref, pairs, sems):
    logits = dot(par[...], tok[...], ((1,), (1,)))
    dispatch = softmax(logits, 1)
    combine = softmax(logits, 0)
    pairs[:, 0, :] = dot(dispatch.astype(BF16), tok[...], ((1,), (0,))).astype(BF16)
    pairs[:, 1, :] = dot(combine.astype(BF16), cot[...], ((1,), (0,))).astype(BF16)
    copies = [pltpu.make_async_copy(pairs, out.at[y], sems.at[y]) for y in range(8)]
    for copy in copies:
        copy.start()
    dispatch_ref[...] = dispatch
    combine_ref[...] = combine
    for copy in copies:
        copy.wait()


def route(tokens, cotangent, params_t):
    hbm = pl.BlockSpec(memory_space=pl.ANY)
    vmem = pl.BlockSpec(memory_space=pltpu.VMEM)
    return pl.pallas_call(
        route_kernel,
        out_shape=(shape((8, 16, 2, 1408), BF16), shape((16, 256), F32), shape((16, 256), F32)),
        in_specs=[vmem, vmem, vmem],
        out_specs=(hbm, vmem, vmem),
        scratch_shapes=[pltpu.VMEM((16, 2, 1408), BF16), pltpu.SemaphoreType.DMA((8,))],
        compiler_params=pltpu.CompilerParams(vmem_limit_bytes=SMALL),
        cost_estimate=pl.CostEstimate(flops=4 * 10**7, bytes_accessed=3 * 10**6, transcendentals=0),
    )(tokens, cotangent, params_t)


def hidden_kernel(*refs):
    routed, weights, outs, scratch = refs[0], refs[1:5], refs[5:11], refs[11:]
    back_out, core_out, act_out, slope_out, x_out, g_out = outs
    rows, lifts, drops, x, g, act, slope, back, core, sems = scratch
    unpack = pltpu.make_async_copy(routed, rows, sems.at[0])
    unpack.start()
    order = (2, 3, 0, 1)
    loads = {}
    for k in order:
        part = pl.ds(192 * k, 192)
        loads[k] = (
            pltpu.make_async_copy(weights[k].at[pl.ds(0, 192)], lifts.at[part], sems.at[1 + 2 * k]),
            pltpu.make_async_copy(weights[k].at[pl.ds(192, 192)], drops.at[part], sems.at[2 + 2 * k]),
        )
        for load in loads[k]:
            load.start()
    stores = []

    def store(src, dst):
        copy = pltpu.make_async_copy(src, dst, sems.at[9 + len(stores)])
        copy.start()
        stores.append(copy)

    unpack.wait()
    for column in range(0, 1408, 128):
        lanes = pl.ds(column, 128)
        both = rows[:, :, lanes].astype(F32)
        x[:, lanes] = both[:, 0, :].astype(BF16)
        g[:, lanes] = both[:, 1, :].astype(BF16)
    store(x, x_out)
    store(g, g_out)
    for k in order:
        for load in loads[k]:
            load.wait()
    for k in order:
        part = pl.ds(192 * k, 192)
        preact = dot(lifts[part, :], x[...], ((1,), (1,)))
        activated_grad = dot(drops[part, :], g[...], ((1,), (1,)))
        rise = 0.5 * (1.0 + lax.erf(preact * 0.7071067811865476))
        bell = preact * jnp.exp(-0.5 * preact * preact) * 0.3989422804014327
        activated = (preact * rise).astype(BF16)
        preact_grad = (activated_grad * (rise + bell)).astype(BF16)
        act[part, :] = activated
        slope[part, :] = preact_grad
        if k >= 2:
            half = pl.ds(384 * (k - 2), 384)
            core[pl.ds(384 * (k - 2), 192), :] = dot(preact_grad, x[...], ((1,), (0,))).astype(BF16)
            core[pl.ds(384 * (k - 2) + 192, 192), :] = dot(
                activated, g[...], ((1,), (0,))
            ).astype(BF16)
            store(core.at[half], core_out.at[half])
    store(act, act_out)
    store(slope, slope_out)
    total = dot(slope[...], lifts[...], ((0,), (0,))).astype(BF16)
    back[:, 0, :] = total[:, :768]
    back[:, 1, :640] = total[:, 768:]
    back[:, 1, 640:] = jnp.zeros((128, 128), BF16)
    store(back, back_out)
    for copy in stores:
        copy.wait()


def fetch(pairs, sems):
    copies = [pltpu.make_async_copy(a, b, sems.at[k]) for k, (a, b) in enumerate(pairs)]
    for copy in copies:
        copy.start()
    return copies


def x_kernel(x_in, g_in, act_in, slope_in, core_in, out_ref, x, g, act, slope, core, sems):
    rows = pl.ds(192, 192)
    copies = fetch(
        (
            (slope_in.at[rows], slope),
            (x_in, x),
            (act_in.at[rows], act),
            (g_in, g),
            (core_in.at[pl.ds(384, 384)], core),
        ),
        sems,
    )
    copies[0].wait()
    copies[1].wait()
    lift = dot(slope[...], x[...], ((1,), (0,)))
    copies[2].wait()
    copies[3].wait()
    drop = dot(act[...], g[...], ((1,), (0,)))
    copies[4].wait()
    out_ref[:192, :] = (lift + core[:192, :].astype(F32)).astype(BF16)
    out_ref[192:, :] = (drop + core[192:, :].astype(F32)).astype(BF16)


def own_kernel(
    x_in, g_in, act_in, slope_in, core_in, over_in, lift_ref, drop_ref,
    x, g, act, slope, core, over, sems,
):
    rows = pl.ds(0, 192)
    copies = fetch(
        (
            (slope_in.at[rows], slope),
            (x_in, x),
            (act_in.at[rows], act),
            (g_in, g),
            (core_in.at[pl.ds(0, 384)], core),
            (over_in, over),
        ),
        sems,
    )
    copies[0].wait()
    copies[1].wait()
    lift = dot(slope[...], x[...], ((1,), (0,)))
    copies[2].wait()
    copies[3].wait()
    drop = dot(act[...], g[...], ((1,), (0,)))
    copies[4].wait()
    copies[5].wait()
    lift_ref[...] = (lift + core[:192, :].astype(F32) + over[:192, :].astype(F32)).astype(BF16)
    drop_ref[...] = (drop + core[192:, :].astype(F32) + over[192:, :].astype(F32)).astype(BF16)


def combine_kernel(out_ref, cot, combine, grad_ref):
    grad = dot(out_ref[...], cot[...], ((1,), (1,)))
    weighted = jnp.sum(grad * combine[...], axis=0, keepdims=True)
    grad_ref[...] = combine[...] * (grad - weighted)


def image_kernel(
    returned, tok, par, dispatch_in, part_in, out, left_ref, right_ref, dispatch, part, sems
):
    loads = fetch(((dispatch_in, dispatch), (part_in, part)), sems)
    head = tail = None
    for y in range(8):
        rows = pl.ds(16 * y, 16)
        one = returned[rows, 0, :].astype(F32)
        two = returned[rows, 1, :].astype(F32)
        head = one if head is None else head + one
        tail = two if tail is None else tail + two
    slot_grad = jnp.concatenate([head, tail[:, :640]], axis=1).astype(BF16)
    right_ref[:16, :] = slot_grad
    right_ref[16:32, :] = par[...]
    right_ref[32:, :] = par[...]
    grad = dot(slot_grad, tok[...], ((1,), (1,)))
    for load in loads:
        load.wait()
    weighted = jnp.sum(grad * dispatch[...], axis=1, keepdims=True)
    logit = part[...] + dispatch[...] * (grad - weighted)
    high = logit.astype(BF16)
    low = (logit - high.astype(F32)).astype(BF16)
    left_ref[:16, :] = dispatch[...].astype(BF16)
    left_ref[16:32, :] = high
    left_ref[32:, :] = low
    local = dot(high, tok[...], ((1,), (0,))) + dot(low, tok[...], ((1,), (0,)))
    local = local.astype(BF16)
    out[:, 0, :] = local[:, :768]
    out[:, 1, :640] = local[:, 768:]
    out[:, 1, 640:] = jnp.zeros((16, 128), BF16)


def shards(tokens, cotangent, slot_outputs, slot_params, lift_weight, drop_weight):
    tokens, cotangent, slot_outputs = tokens[0], cotangent[0], slot_outputs[0]
    lift, drop = lift_weight[0], drop_weight[0]
    own = call(
        join_kernel,
        (shape((384, 1408), BF16),),
        (lift, drop),
        0,
        hbm=True,
        scratch=[pltpu.SemaphoreType.DMA((2,))],
    )[0]
    over_x = hold(lax.ppermute(own, "xhi", SWAP))
    over_both = lax.ppermute(over_x, "core", SWAP)

    params_t = slot_params.T
    sent, dispatch, combine = route(tokens, cotangent, params_t)
    combine, own = lax.optimization_barrier((combine, own))
    over_core = lax.ppermute(own, "core", SWAP)
    routed = exchange(sent.reshape(128, 2, 1408), HIDDEN)
    combine_part = call(
        combine_kernel,
        (shape((16, 256), F32),),
        (slot_outputs, cotangent, combine),
        16 * 256 * 1408,
    )[0]

    routed, combine_part = lax.optimization_barrier((routed, combine_part))
    units = shape((768, 128), BF16)
    images = shape((128, 1408), BF16)
    core_half = shape((768, 1408), BF16)
    folded = shape((128, 2, 768), BF16)
    backward, to_core, activated, slopes, inputs, upstream = call(
        hidden_kernel,
        (folded, core_half, units, units, images, images),
        (routed, own, over_x, over_core, over_both),
        5 * 128 * 768 * 1408,
        hbm=True,
        scratch=[
            pltpu.VMEM(a.shape, BF16)
            for a in (
                routed, core_half, core_half, images, images, units, units, folded, core_half
            )
        ]
        + [pltpu.SemaphoreType.DMA((16,))],
    )
    returned = exchange(backward, HIDDEN)
    rows = (inputs, upstream, activated, slopes)
    from_core = lax.ppermute(to_core, "core", SWAP)
    vmem = pl.BlockSpec(memory_space=pltpu.VMEM)
    quarter = [
        pltpu.VMEM(size, BF16) for size in ((128, 1408),) * 2 + ((192, 128),) * 2 + ((384, 1408),)
    ]
    to_x = call(
        x_kernel,
        (shape((384, 1408), BF16),),
        rows + (from_core,),
        2 * 192 * 128 * 1408,
        hbm=True,
        out_place=vmem,
        scratch=quarter + [pltpu.SemaphoreType.DMA((5,))],
    )[0]
    from_x = lax.ppermute(to_x, "xhi", SWAP)
    returned, to_x = lax.optimization_barrier((returned, to_x))
    half = shape((192, 1408), BF16)
    lift_grad, drop_grad = call(
        own_kernel,
        (half, half),
        rows + (from_core, from_x),
        2 * 192 * 128 * 1408,
        hbm=True,
        out_place=vmem,
        scratch=quarter + quarter[4:] + [pltpu.SemaphoreType.DMA((6,))],
    )

    local, left, right = pl.pallas_call(
        image_kernel,
        out_shape=(shape((16, 2, 768), BF16), shape((48, 256), BF16), shape((48, 1408), BF16)),
        in_specs=[vmem] * 3 + [pl.BlockSpec(memory_space=pl.ANY)] * 2,
        out_specs=(vmem,) * 3,
        scratch_shapes=[pltpu.VMEM((16, 256), F32)] * 2 + [pltpu.SemaphoreType.DMA((2,))],
        compiler_params=pltpu.CompilerParams(vmem_limit_bytes=SMALL),
        cost_estimate=pl.CostEstimate(flops=4 * 10**7, bytes_accessed=2 * 10**6, transcendentals=0),
    )(returned, tokens, params_t, dispatch, combine_part)
    by_slot = exchange(local, NEAR)
    by_slot = jnp.sum(by_slot.astype(F32), axis=0).astype(BF16)
    by_group = exchange(jnp.broadcast_to(by_slot[None], (32, 2, 768)), FAR)
    total = jnp.sum(by_group.astype(F32), axis=0).astype(BF16)
    columns = exchange(jnp.broadcast_to(total[None], (16, 2, 768)), NEAR)
    columns, lift_grad, drop_grad = lax.optimization_barrier((columns, lift_grad, drop_grad))
    param_grad = jnp.concatenate([columns[:, 0, :], columns[:, 1, :640]], axis=1).astype(F32).T

    token_grad = jnp.einsum("kp,kd->pd", left, right, preferred_element_type=F32).astype(BF16)
    return (token_grad[None], param_grad, lift_grad[None], drop_grad[None])


def solution(mesh):
    split = Mesh(mesh.devices.reshape(2, 8, 2, 8, 2), AXES)
    images = P(AXES, None, None)
    hidden = P(EXPERT, DP, None)
    return jax.shard_map(
        shards,
        mesh=split,
        in_specs=(images, images, images, P(), hidden, hidden),
        out_specs=(images, P(), hidden, hidden),
        check_vma=False,
    )
```

```python
import jax
import jax.numpy as jnp
from jax import lax
from jax.experimental import pallas as pl
from jax.experimental.pallas import tpu as pltpu
from jax.sharding import Mesh, PartitionSpec as P

AXES = ("xhi", "y", "core", "z", "xlo")
DP = ("xhi", "y", "core")
NEAR = ("core", "z")
FAR = ("xhi", "y", "xlo")
EXPERT = ("z", "xlo")
HIDDEN = ("y", "z", "xlo")
SWAP = [(0, 1), (1, 0)]
BF16 = jnp.bfloat16
F32 = jnp.float32
LIMIT = 56 * 2**20
SMALL = 24 * 2**20
shape = jax.ShapeDtypeStruct


def dot(a, b, contract):
    return lax.dot_general(a, b, (contract, ((), ())), preferred_element_type=F32)


def call(kernel, out, args, macs, hbm=False, scratch=(), aliases={}, limit=LIMIT, out_place=None):
    place = pl.ANY if hbm else pltpu.VMEM
    return pl.pallas_call(
        kernel,
        out_shape=out,
        in_specs=[pl.BlockSpec(memory_space=place) for a in args],
        out_specs=jax.tree.map(lambda _: out_place or pl.BlockSpec(memory_space=place), out),
        scratch_shapes=scratch,
        input_output_aliases=aliases,
        compiler_params=pltpu.CompilerParams(vmem_limit_bytes=limit),
        cost_estimate=pl.CostEstimate(
            flops=2 * macs,
            bytes_accessed=sum(a.size * a.dtype.itemsize for a in list(args) + list(out)),
            transcendentals=0,
        ),
    )(*args)


def join_kernel(lift, drop, out, rows, sems):
    top, bottom = pl.ds(0, 192), pl.ds(192, 192)
    loads = fetch(((lift, rows.at[top]), (drop, rows.at[bottom])), sems)
    stores = []
    for k, part in enumerate((top, bottom)):
        loads[k].wait()
        stores.append(pltpu.make_async_copy(rows.at[part], out.at[part], sems.at[2 + k]))
        stores[k].start()
    for store in stores:
        store.wait()


def hold_kernel(src_ref, dst_ref):
    pass


def hold(value):
    return call(
        hold_kernel, (value,), (value,), 10**10, hbm=True, aliases={0: 0}, limit=SMALL
    )[0]


def exchange(blocks, axes):
    return lax.all_to_all(blocks, axes, split_axis=0, concat_axis=0, tiled=True)


def softmax(values, axis):
    top = jnp.exp(values - jnp.max(values, axis=axis, keepdims=True))
    return top / jnp.sum(top, axis=axis, keepdims=True)


def route_kernel(tok, cot, par, out, dispatch_ref, combine_ref, pairs, sems):
    logits = dot(par[...], tok[...], ((1,), (1,)))
    dispatch = softmax(logits, 1)
    combine = softmax(logits, 0)
    pairs[:, 0, :] = dot(dispatch.astype(BF16), tok[...], ((1,), (0,))).astype(BF16)
    pairs[:, 1, :] = dot(combine.astype(BF16), cot[...], ((1,), (0,))).astype(BF16)
    copies = [pltpu.make_async_copy(pairs, out.at[y], sems.at[y]) for y in range(8)]
    for copy in copies:
        copy.start()
    dispatch_ref[...] = dispatch
    combine_ref[...] = combine
    for copy in copies:
        copy.wait()


def route(tokens, cotangent, params_t):
    hbm = pl.BlockSpec(memory_space=pl.ANY)
    vmem = pl.BlockSpec(memory_space=pltpu.VMEM)
    return pl.pallas_call(
        route_kernel,
        out_shape=(shape((8, 16, 2, 1408), BF16), shape((16, 256), F32), shape((16, 256), F32)),
        in_specs=[vmem, vmem, vmem],
        out_specs=(hbm, vmem, vmem),
        scratch_shapes=[pltpu.VMEM((16, 2, 1408), BF16), pltpu.SemaphoreType.DMA((8,))],
        compiler_params=pltpu.CompilerParams(vmem_limit_bytes=SMALL),
        cost_estimate=pl.CostEstimate(flops=4 * 10**7, bytes_accessed=3 * 10**6, transcendentals=0),
    )(tokens, cotangent, params_t)


def hidden_kernel(*refs):
    routed, weights, outs, scratch = refs[0], refs[1:5], refs[5:11], refs[11:]
    back_out, core_out, act_out, slope_out, x_out, g_out = outs
    rows, lifts, drops, x, g, act, slope, back, core, sems = scratch
    unpack = pltpu.make_async_copy(routed, rows, sems.at[0])
    unpack.start()
    order = (2, 3, 0, 1)
    loads = {}
    for k in order:
        part = pl.ds(192 * k, 192)
        loads[k] = (
            pltpu.make_async_copy(weights[k].at[pl.ds(0, 192)], lifts.at[part], sems.at[1 + 2 * k]),
            pltpu.make_async_copy(weights[k].at[pl.ds(192, 192)], drops.at[part], sems.at[2 + 2 * k]),
        )
        for load in loads[k]:
            load.start()
    stores = []

    def store(src, dst):
        copy = pltpu.make_async_copy(src, dst, sems.at[9 + len(stores)])
        copy.start()
        stores.append(copy)

    unpack.wait()
    for column in range(0, 1408, 128):
        lanes = pl.ds(column, 128)
        both = rows[:, :, lanes].astype(F32)
        x[:, lanes] = both[:, 0, :].astype(BF16)
        g[:, lanes] = both[:, 1, :].astype(BF16)
    store(x, x_out)
    store(g, g_out)
    for k in order:
        for load in loads[k]:
            load.wait()
    for k in order:
        part = pl.ds(192 * k, 192)
        preact = dot(lifts[part, :], x[...], ((1,), (1,)))
        activated_grad = dot(drops[part, :], g[...], ((1,), (1,)))
        rise = 0.5 * (1.0 + lax.erf(preact * 0.7071067811865476))
        bell = preact * jnp.exp(-0.5 * preact * preact) * 0.3989422804014327
        activated = (preact * rise).astype(BF16)
        preact_grad = (activated_grad * (rise + bell)).astype(BF16)
        act[part, :] = activated
        slope[part, :] = preact_grad
        if k >= 2:
            half = pl.ds(384 * (k - 2), 384)
            core[pl.ds(384 * (k - 2), 192), :] = dot(preact_grad, x[...], ((1,), (0,))).astype(BF16)
            core[pl.ds(384 * (k - 2) + 192, 192), :] = dot(
                activated, g[...], ((1,), (0,))
            ).astype(BF16)
            store(core.at[half], core_out.at[half])
    store(act, act_out)
    store(slope, slope_out)
    total = dot(slope[...], lifts[...], ((0,), (0,))).astype(BF16)
    back[:, 0, :] = total[:, :768]
    back[:, 1, :640] = total[:, 768:]
    back[:, 1, 640:] = jnp.zeros((128, 128), BF16)
    store(back, back_out)
    for copy in stores:
        copy.wait()


def fetch(pairs, sems):
    copies = [pltpu.make_async_copy(a, b, sems.at[k]) for k, (a, b) in enumerate(pairs)]
    for copy in copies:
        copy.start()
    return copies


def x_kernel(x_in, g_in, act_in, slope_in, core_in, out_ref, x, g, act, slope, core, sems):
    rows = pl.ds(192, 192)
    copies = fetch(
        (
            (slope_in.at[rows], slope),
            (x_in, x),
            (act_in.at[rows], act),
            (g_in, g),
            (core_in.at[pl.ds(384, 384)], core),
        ),
        sems,
    )
    copies[0].wait()
    copies[1].wait()
    lift = dot(slope[...], x[...], ((1,), (0,)))
    copies[2].wait()
    copies[3].wait()
    drop = dot(act[...], g[...], ((1,), (0,)))
    copies[4].wait()
    out_ref[:192, :] = (lift + core[:192, :].astype(F32)).astype(BF16)
    out_ref[192:, :] = (drop + core[192:, :].astype(F32)).astype(BF16)


def own_kernel(
    x_in, g_in, act_in, slope_in, core_in, over_in, lift_ref, drop_ref,
    x, g, act, slope, core, over, sems,
):
    rows = pl.ds(0, 192)
    copies = fetch(
        (
            (slope_in.at[rows], slope),
            (x_in, x),
            (act_in.at[rows], act),
            (g_in, g),
            (core_in.at[pl.ds(0, 384)], core),
            (over_in, over),
        ),
        sems,
    )
    copies[0].wait()
    copies[1].wait()
    lift = dot(slope[...], x[...], ((1,), (0,)))
    copies[2].wait()
    copies[3].wait()
    drop = dot(act[...], g[...], ((1,), (0,)))
    copies[4].wait()
    copies[5].wait()
    lift_ref[...] = (lift + core[:192, :].astype(F32) + over[:192, :].astype(F32)).astype(BF16)
    drop_ref[...] = (drop + core[192:, :].astype(F32) + over[192:, :].astype(F32)).astype(BF16)


def combine_kernel(out_ref, cot, combine, grad_ref):
    grad = dot(out_ref[...], cot[...], ((1,), (1,)))
    weighted = jnp.sum(grad * combine[...], axis=0, keepdims=True)
    grad_ref[...] = combine[...] * (grad - weighted)


def image_kernel(
    returned, tok, par, dispatch_in, part_in, out, left_ref, right_ref, dispatch, part, sems
):
    loads = fetch(((dispatch_in, dispatch), (part_in, part)), sems)
    head = tail = None
    for y in range(8):
        rows = pl.ds(16 * y, 16)
        one = returned[rows, 0, :].astype(F32)
        two = returned[rows, 1, :].astype(F32)
        head = one if head is None else head + one
        tail = two if tail is None else tail + two
    slot_grad = jnp.concatenate([head, tail[:, :640]], axis=1).astype(BF16)
    right_ref[:16, :] = slot_grad
    right_ref[16:32, :] = par[...]
    right_ref[32:, :] = par[...]
    grad = dot(slot_grad, tok[...], ((1,), (1,)))
    for load in loads:
        load.wait()
    weighted = jnp.sum(grad * dispatch[...], axis=1, keepdims=True)
    logit = part[...] + dispatch[...] * (grad - weighted)
    high = logit.astype(BF16)
    low = (logit - high.astype(F32)).astype(BF16)
    left_ref[:16, :] = dispatch[...].astype(BF16)
    left_ref[16:32, :] = high
    left_ref[32:, :] = low
    local = dot(high, tok[...], ((1,), (0,))) + dot(low, tok[...], ((1,), (0,)))
    local = local.astype(BF16)
    out[:, 0, :] = local[:, :768]
    out[:, 1, :640] = local[:, 768:]
    out[:, 1, 640:] = jnp.zeros((16, 128), BF16)


def shards(tokens, cotangent, slot_outputs, slot_params, lift_weight, drop_weight):
    tokens, cotangent, slot_outputs = tokens[0], cotangent[0], slot_outputs[0]
    lift, drop = lift_weight[0], drop_weight[0]
    own = call(
        join_kernel,
        (shape((384, 1408), BF16),),
        (lift, drop),
        0,
        hbm=True,
        scratch=[pltpu.VMEM((384, 1408), BF16), pltpu.SemaphoreType.DMA((4,))],
    )[0]
    over_x = hold(lax.ppermute(own, "xhi", SWAP))
    over_both = lax.ppermute(over_x, "core", SWAP)

    params_t = slot_params.T
    sent, dispatch, combine = route(tokens, cotangent, params_t)
    combine, own = lax.optimization_barrier((combine, own))
    over_core = lax.ppermute(own, "core", SWAP)
    routed = exchange(sent.reshape(128, 2, 1408), HIDDEN)
    combine_part = call(
        combine_kernel,
        (shape((16, 256), F32),),
        (slot_outputs, cotangent, combine),
        16 * 256 * 1408,
    )[0]

    routed, combine_part = lax.optimization_barrier((routed, combine_part))
    units = shape((768, 128), BF16)
    images = shape((128, 1408), BF16)
    core_half = shape((768, 1408), BF16)
    folded = shape((128, 2, 768), BF16)
    backward, to_core, activated, slopes, inputs, upstream = call(
        hidden_kernel,
        (folded, core_half, units, units, images, images),
        (routed, own, over_x, over_core, over_both),
        5 * 128 * 768 * 1408,
        hbm=True,
        scratch=[
            pltpu.VMEM(a.shape, BF16)
            for a in (
                routed, core_half, core_half, images, images, units, units, folded, core_half
            )
        ]
        + [pltpu.SemaphoreType.DMA((16,))],
    )
    returned = exchange(backward, HIDDEN)
    rows = (inputs, upstream, activated, slopes)
    from_core = lax.ppermute(to_core, "core", SWAP)
    vmem = pl.BlockSpec(memory_space=pltpu.VMEM)
    quarter = [
        pltpu.VMEM(size, BF16) for size in ((128, 1408),) * 2 + ((192, 128),) * 2 + ((384, 1408),)
    ]
    to_x = call(
        x_kernel,
        (shape((384, 1408), BF16),),
        rows + (from_core,),
        2 * 192 * 128 * 1408,
        hbm=True,
        out_place=vmem,
        scratch=quarter + [pltpu.SemaphoreType.DMA((5,))],
    )[0]
    from_x = lax.ppermute(to_x, "xhi", SWAP)
    returned, to_x = lax.optimization_barrier((returned, to_x))
    half = shape((192, 1408), BF16)
    lift_grad, drop_grad = call(
        own_kernel,
        (half, half),
        rows + (from_core, from_x),
        2 * 192 * 128 * 1408,
        hbm=True,
        out_place=vmem,
        scratch=quarter + quarter[4:] + [pltpu.SemaphoreType.DMA((6,))],
    )

    local, left, right = pl.pallas_call(
        image_kernel,
        out_shape=(shape((16, 2, 768), BF16), shape((48, 256), BF16), shape((48, 1408), BF16)),
        in_specs=[vmem] * 3 + [pl.BlockSpec(memory_space=pl.ANY)] * 2,
        out_specs=(vmem,) * 3,
        scratch_shapes=[pltpu.VMEM((16, 256), F32)] * 2 + [pltpu.SemaphoreType.DMA((2,))],
        compiler_params=pltpu.CompilerParams(vmem_limit_bytes=SMALL),
        cost_estimate=pl.CostEstimate(flops=4 * 10**7, bytes_accessed=2 * 10**6, transcendentals=0),
    )(returned, tokens, params_t, dispatch, combine_part)
    by_slot = exchange(local, NEAR)
    by_slot = jnp.sum(by_slot.astype(F32), axis=0).astype(BF16)
    by_group = exchange(jnp.broadcast_to(by_slot[None], (32, 2, 768)), FAR)
    total = jnp.sum(by_group.astype(F32), axis=0).astype(BF16)
    columns = exchange(jnp.broadcast_to(total[None], (16, 2, 768)), NEAR)
    columns, lift_grad, drop_grad = lax.optimization_barrier((columns, lift_grad, drop_grad))
    param_grad = jnp.concatenate([columns[:, 0, :], columns[:, 1, :640]], axis=1).astype(F32).T

    token_grad = jnp.einsum("kp,kd->pd", left, right, preferred_element_type=F32).astype(BF16)
    return (token_grad[None], param_grad, lift_grad[None], drop_grad[None])


def solution(mesh):
    split = Mesh(mesh.devices.reshape(2, 8, 2, 8, 2), AXES)
    images = P(AXES, None, None)
    hidden = P(EXPERT, DP, None)
    return jax.shard_map(
        shards,
        mesh=split,
        in_specs=(images, images, images, P(), hidden, hidden),
        out_specs=(images, P(), hidden, hidden),
        check_vma=False,
    )
```

```python
import jax
import jax.numpy as jnp
from jax import lax
from jax.experimental import pallas as pl
from jax.experimental.pallas import tpu as pltpu
from jax.sharding import Mesh, PartitionSpec as P

AXES = ("xhi", "y", "core", "z", "xlo")
DP = ("xhi", "y", "core")
NEAR = ("core", "z")
FAR = ("xhi", "y", "xlo")
EXPERT = ("z", "xlo")
HIDDEN = ("y", "z", "xlo")
SWAP = [(0, 1), (1, 0)]
BF16 = jnp.bfloat16
F32 = jnp.float32
LIMIT = 56 * 2**20
SMALL = 24 * 2**20
shape = jax.ShapeDtypeStruct


def dot(a, b, contract):
    return lax.dot_general(a, b, (contract, ((), ())), preferred_element_type=F32)


def call(kernel, out, args, macs, hbm=False, scratch=(), aliases={}, limit=LIMIT, out_place=None):
    place = pl.ANY if hbm else pltpu.VMEM
    return pl.pallas_call(
        kernel,
        out_shape=out,
        in_specs=[pl.BlockSpec(memory_space=place) for a in args],
        out_specs=jax.tree.map(lambda _: out_place or pl.BlockSpec(memory_space=place), out),
        scratch_shapes=scratch,
        input_output_aliases=aliases,
        compiler_params=pltpu.CompilerParams(vmem_limit_bytes=limit),
        cost_estimate=pl.CostEstimate(
            flops=2 * macs,
            bytes_accessed=sum(a.size * a.dtype.itemsize for a in list(args) + list(out)),
            transcendentals=0,
        ),
    )(*args)


def join_kernel(lift, drop, out, rows, sems):
    top, bottom = pl.ds(0, 192), pl.ds(192, 192)
    loads = fetch(((lift, rows.at[top]), (drop, rows.at[bottom])), sems)
    stores = []
    for k, part in enumerate((top, bottom)):
        loads[k].wait()
        stores.append(pltpu.make_async_copy(rows.at[part], out.at[part], sems.at[2 + k]))
        stores[k].start()
    for store in stores:
        store.wait()


def hold_kernel(src_ref, dst_ref):
    pass


def hold(value):
    return call(
        hold_kernel, (value,), (value,), 10**10, hbm=True, aliases={0: 0}, limit=SMALL
    )[0]


def exchange(blocks, axes):
    return lax.all_to_all(blocks, axes, split_axis=0, concat_axis=0, tiled=True)


def softmax(values, axis):
    top = jnp.exp(values - jnp.max(values, axis=axis, keepdims=True))
    return top / jnp.sum(top, axis=axis, keepdims=True)


def route_kernel(tok, cot, par, out, dispatch_ref, combine_ref, pairs, sems):
    logits = dot(par[...], tok[...], ((1,), (1,)))
    dispatch = softmax(logits, 1)
    combine = softmax(logits, 0)
    pairs[:, 0, :] = dot(dispatch.astype(BF16), tok[...], ((1,), (0,))).astype(BF16)
    pairs[:, 1, :] = dot(combine.astype(BF16), cot[...], ((1,), (0,))).astype(BF16)
    copies = [pltpu.make_async_copy(pairs, out.at[y], sems.at[y]) for y in range(8)]
    for copy in copies:
        copy.start()
    dispatch_ref[...] = dispatch
    combine_ref[...] = combine
    for copy in copies:
        copy.wait()


def route(tokens, cotangent, params_t):
    hbm = pl.BlockSpec(memory_space=pl.ANY)
    vmem = pl.BlockSpec(memory_space=pltpu.VMEM)
    return pl.pallas_call(
        route_kernel,
        out_shape=(shape((8, 16, 2, 1408), BF16), shape((16, 256), F32), shape((16, 256), F32)),
        in_specs=[vmem, vmem, vmem],
        out_specs=(hbm, vmem, vmem),
        scratch_shapes=[pltpu.VMEM((16, 2, 1408), BF16), pltpu.SemaphoreType.DMA((8,))],
        compiler_params=pltpu.CompilerParams(vmem_limit_bytes=SMALL),
        cost_estimate=pl.CostEstimate(flops=4 * 10**7, bytes_accessed=3 * 10**6, transcendentals=0),
    )(tokens, cotangent, params_t)


def hidden_kernel(*refs):
    routed, weights, outs, scratch = refs[0], refs[1:5], refs[5:11], refs[11:]
    back_out, core_out, act_out, slope_out, x_out, g_out = outs
    rows, lifts, drops, x, g, act, slope, back, core, sems = scratch
    unpack = pltpu.make_async_copy(routed, rows, sems.at[0])
    unpack.start()
    order = (2, 3, 0, 1)
    loads = {}
    for k in order:
        part = pl.ds(192 * k, 192)
        loads[k] = (
            pltpu.make_async_copy(weights[k].at[pl.ds(0, 192)], lifts.at[part], sems.at[1 + 2 * k]),
            pltpu.make_async_copy(weights[k].at[pl.ds(192, 192)], drops.at[part], sems.at[2 + 2 * k]),
        )
        for load in loads[k]:
            load.start()
    stores = []

    def store(src, dst):
        copy = pltpu.make_async_copy(src, dst, sems.at[9 + len(stores)])
        copy.start()
        stores.append(copy)

    unpack.wait()
    for column in range(0, 1408, 128):
        lanes = pl.ds(column, 128)
        both = rows[:, :, lanes].astype(F32)
        x[:, lanes] = both[:, 0, :].astype(BF16)
        g[:, lanes] = both[:, 1, :].astype(BF16)
    store(x, x_out)
    store(g, g_out)
    for k in order:
        for load in loads[k]:
            load.wait()
    for k in order:
        part = pl.ds(192 * k, 192)
        preact = dot(lifts[part, :], x[...], ((1,), (1,)))
        activated_grad = dot(drops[part, :], g[...], ((1,), (1,)))
        rise = 0.5 * (1.0 + lax.erf(preact * 0.7071067811865476))
        bell = preact * jnp.exp(-0.5 * preact * preact) * 0.3989422804014327
        activated = (preact * rise).astype(BF16)
        preact_grad = (activated_grad * (rise + bell)).astype(BF16)
        act[part, :] = activated
        slope[part, :] = preact_grad
        if k >= 2:
            half = pl.ds(384 * (k - 2), 384)
            core[pl.ds(384 * (k - 2), 192), :] = dot(preact_grad, x[...], ((1,), (0,))).astype(BF16)
            core[pl.ds(384 * (k - 2) + 192, 192), :] = dot(
                activated, g[...], ((1,), (0,))
            ).astype(BF16)
            store(core.at[half], core_out.at[half])
    store(act, act_out)
    store(slope, slope_out)
    total = dot(slope[...], lifts[...], ((0,), (0,))).astype(BF16)
    back[:, 0, :] = total[:, :768]
    back[:, 1, :640] = total[:, 768:]
    back[:, 1, 640:] = jnp.zeros((128, 128), BF16)
    store(back, back_out)
    for copy in stores:
        copy.wait()


def fetch(pairs, sems):
    copies = [pltpu.make_async_copy(a, b, sems.at[k]) for k, (a, b) in enumerate(pairs)]
    for copy in copies:
        copy.start()
    return copies


def x_kernel(x_in, g_in, act_in, slope_in, core_in, out_ref, x, g, act, slope, core, sems):
    rows = pl.ds(192, 192)
    copies = fetch(
        (
            (slope_in.at[rows], slope),
            (x_in, x),
            (act_in.at[rows], act),
            (g_in, g),
            (core_in.at[pl.ds(384, 384)], core),
        ),
        sems,
    )
    copies[0].wait()
    copies[1].wait()
    lift = dot(slope[...], x[...], ((1,), (0,)))
    copies[2].wait()
    copies[3].wait()
    drop = dot(act[...], g[...], ((1,), (0,)))
    copies[4].wait()
    out_ref[:192, :] = (lift + core[:192, :].astype(F32)).astype(BF16)
    out_ref[192:, :] = (drop + core[192:, :].astype(F32)).astype(BF16)


def own_kernel(
    x_in, g_in, act_in, slope_in, core_in, over_in, lift_ref, drop_ref,
    x, g, act, slope, core, over, sems,
):
    rows = pl.ds(0, 192)
    copies = fetch(
        (
            (slope_in.at[rows], slope),
            (x_in, x),
            (act_in.at[rows], act),
            (g_in, g),
            (core_in.at[pl.ds(0, 384)], core),
            (over_in, over),
        ),
        sems,
    )
    copies[0].wait()
    copies[1].wait()
    lift = dot(slope[...], x[...], ((1,), (0,)))
    copies[2].wait()
    copies[3].wait()
    drop = dot(act[...], g[...], ((1,), (0,)))
    copies[4].wait()
    copies[5].wait()
    lift_ref[...] = (lift + core[:192, :].astype(F32) + over[:192, :].astype(F32)).astype(BF16)
    drop_ref[...] = (drop + core[192:, :].astype(F32) + over[192:, :].astype(F32)).astype(BF16)


def combine_kernel(out_ref, cot, combine, grad_ref):
    grad = dot(out_ref[...], cot[...], ((1,), (1,)))
    weighted = jnp.sum(grad * combine[...], axis=0, keepdims=True)
    grad_ref[...] = combine[...] * (grad - weighted)


def image_kernel(
    returned, tok, par, dispatch_in, part_in, out, left_ref, right_ref, dispatch, part, sems
):
    loads = fetch(((dispatch_in, dispatch), (part_in, part)), sems)
    head = tail = None
    for y in range(8):
        rows = pl.ds(16 * y, 16)
        one = returned[rows, 0, :].astype(F32)
        two = returned[rows, 1, :].astype(F32)
        head = one if head is None else head + one
        tail = two if tail is None else tail + two
    slot_grad = jnp.concatenate([head, tail[:, :640]], axis=1).astype(BF16)
    right_ref[:16, :] = slot_grad
    right_ref[16:32, :] = par[...]
    right_ref[32:, :] = par[...]
    grad = dot(slot_grad, tok[...], ((1,), (1,)))
    for load in loads:
        load.wait()
    weighted = jnp.sum(grad * dispatch[...], axis=1, keepdims=True)
    logit = part[...] + dispatch[...] * (grad - weighted)
    high = logit.astype(BF16)
    low = (logit - high.astype(F32)).astype(BF16)
    left_ref[:16, :] = dispatch[...].astype(BF16)
    left_ref[16:32, :] = high
    left_ref[32:, :] = low
    local = dot(high, tok[...], ((1,), (0,))) + dot(low, tok[...], ((1,), (0,)))
    local = local.astype(BF16)
    out[:, 0, :] = local[:, :768]
    out[:, 1, :640] = local[:, 768:]
    out[:, 1, 640:] = jnp.zeros((16, 128), BF16)


def shards(tokens, cotangent, slot_outputs, slot_params, lift_weight, drop_weight):
    tokens, cotangent, slot_outputs = tokens[0], cotangent[0], slot_outputs[0]
    lift, drop = lift_weight[0], drop_weight[0]
    own = call(
        join_kernel,
        (shape((384, 1408), BF16),),
        (lift, drop),
        0,
        hbm=True,
        scratch=[pltpu.VMEM((384, 1408), BF16), pltpu.SemaphoreType.DMA((4,))],
        limit=SMALL,
    )[0]
    over_x = hold(lax.ppermute(own, "xhi", SWAP))
    over_both = lax.ppermute(over_x, "core", SWAP)

    params_t = slot_params.T
    sent, dispatch, combine = route(tokens, cotangent, params_t)
    combine, own = lax.optimization_barrier((combine, own))
    over_core = lax.ppermute(own, "core", SWAP)
    routed = exchange(sent.reshape(128, 2, 1408), HIDDEN)
    combine_part = call(
        combine_kernel,
        (shape((16, 256), F32),),
        (slot_outputs, cotangent, combine),
        16 * 256 * 1408,
    )[0]

    routed, combine_part = lax.optimization_barrier((routed, combine_part))
    units = shape((768, 128), BF16)
    images = shape((128, 1408), BF16)
    core_half = shape((768, 1408), BF16)
    folded = shape((128, 2, 768), BF16)
    backward, to_core, activated, slopes, inputs, upstream = call(
        hidden_kernel,
        (folded, core_half, units, units, images, images),
        (routed, own, over_x, over_core, over_both),
        5 * 128 * 768 * 1408,
        hbm=True,
        scratch=[
            pltpu.VMEM(a.shape, BF16)
            for a in (
                routed, core_half, core_half, images, images, units, units, folded, core_half
            )
        ]
        + [pltpu.SemaphoreType.DMA((16,))],
    )
    returned = exchange(backward, HIDDEN)
    rows = (inputs, upstream, activated, slopes)
    from_core = lax.ppermute(to_core, "core", SWAP)
    vmem = pl.BlockSpec(memory_space=pltpu.VMEM)
    quarter = [
        pltpu.VMEM(size, BF16) for size in ((128, 1408),) * 2 + ((192, 128),) * 2 + ((384, 1408),)
    ]
    to_x = call(
        x_kernel,
        (shape((384, 1408), BF16),),
        rows + (from_core,),
        2 * 192 * 128 * 1408,
        hbm=True,
        out_place=vmem,
        scratch=quarter + [pltpu.SemaphoreType.DMA((5,))],
    )[0]
    from_x = lax.ppermute(to_x, "xhi", SWAP)
    returned, to_x = lax.optimization_barrier((returned, to_x))
    half = shape((192, 1408), BF16)
    lift_grad, drop_grad = call(
        own_kernel,
        (half, half),
        rows + (from_core, from_x),
        2 * 192 * 128 * 1408,
        hbm=True,
        out_place=vmem,
        scratch=quarter + quarter[4:] + [pltpu.SemaphoreType.DMA((6,))],
    )

    local, left, right = pl.pallas_call(
        image_kernel,
        out_shape=(shape((16, 2, 768), BF16), shape((48, 256), BF16), shape((48, 1408), BF16)),
        in_specs=[vmem] * 3 + [pl.BlockSpec(memory_space=pl.ANY)] * 2,
        out_specs=(vmem,) * 3,
        scratch_shapes=[pltpu.VMEM((16, 256), F32)] * 2 + [pltpu.SemaphoreType.DMA((2,))],
        compiler_params=pltpu.CompilerParams(vmem_limit_bytes=SMALL),
        cost_estimate=pl.CostEstimate(flops=4 * 10**7, bytes_accessed=2 * 10**6, transcendentals=0),
    )(returned, tokens, params_t, dispatch, combine_part)
    by_slot = exchange(local, NEAR)
    by_slot = jnp.sum(by_slot.astype(F32), axis=0).astype(BF16)
    by_group = exchange(jnp.broadcast_to(by_slot[None], (32, 2, 768)), FAR)
    total = jnp.sum(by_group.astype(F32), axis=0).astype(BF16)
    columns = exchange(jnp.broadcast_to(total[None], (16, 2, 768)), NEAR)
    columns, lift_grad, drop_grad = lax.optimization_barrier((columns, lift_grad, drop_grad))
    param_grad = jnp.concatenate([columns[:, 0, :], columns[:, 1, :640]], axis=1).astype(F32).T

    token_grad = jnp.einsum("kp,kd->pd", left, right, preferred_element_type=F32).astype(BF16)
    return (token_grad[None], param_grad, lift_grad[None], drop_grad[None])


def solution(mesh):
    split = Mesh(mesh.devices.reshape(2, 8, 2, 8, 2), AXES)
    images = P(AXES, None, None)
    hidden = P(EXPERT, DP, None)
    return jax.shard_map(
        shards,
        mesh=split,
        in_specs=(images, images, images, P(), hidden, hidden),
        out_specs=(images, P(), hidden, hidden),
        check_vma=False,
    )
```
